1024 devices in a mesh: dp: 128 (over z, x, core), expert: 8 (over y).
Axes of the slice: x: 8, y: 8, z: 8, core: 2. Of those that a mesh axis runs over, the one named last changes fastest.
Arguments:
- tokens: bfloat16 [131072, 1024], P(('dp', 'expert')), may hold values from -6 to 6
- routes: int32 [131072, 2], P(('dp', 'expert')), may hold values from 0 to 7, all different within a row; in each aligned block of 128 rows (0 to 127, 128 to 255, ...) at most 64 rows name the same one
- cotangents: bfloat16 [131072, 2, 704], P(('dp', 'expert')), may hold values from -6 to 6
- momentum: float32 [1024, 5632], P('dp', 'expert'), may hold values from -1024 to 1024
Outputs:
- new_momentum: float32 [1024, 5632], P('dp', 'expert')
- update: float32 [1024, 5632], P('dp', 'expert')
The draws below stay inside these ranges and needn't reach their ends.
Inputs may be any that keep to these rules, and one draw needn't show every extreme that they name: `routes`: each token names 2 different experts; among the 128 tokens of one device no expert is named more than 64 times.
All inputs are finite; a program needn't handle non-finite values.
Results may differ from the reference program's by a relative error of at most 0.002.
The reference program's roundings to bfloat16 on the way (of `nesterov`, `iterate`, `polynomial` and `halfway`) count: a program that leaves them out, or rounds other values in their place, can miss the bound.
Values may be sent and summed in bfloat16 or wider, within the bound.
No kernel may reach another device: no remote copies, remote signals or barrier semaphores. Data moves between devices by JAX's collectives and lax.ppermute only.
A program may use at most 32 MiB of HBM per device.

```python
import math
import jax
import jax.numpy as jnp
import numpy as np
from jax import lax

DW = 1024
HID = 704
TOPK = 2
ITERS = 2
TOK = 128
EXPERTS = 8
CAP = 64
TOKENS = 131072
N_DP = 128


def shard_levels(key, dims, pieces, low, top_value):
    level = 1.0
    for position, parts in pieces:
        draws = jax.random.uniform(jax.random.fold_in(jax.random.fold_in(key, 6), position), (parts,), jnp.float32, low / len(pieces), top_value / len(pieces))
        level = level * jnp.repeat(jnp.exp(draws), dims[position] // parts).reshape((-1,) + (1,) * (len(dims) - 1 - position))
    return level


def deal_out(stream_key, own, number, rows, amount, top, reach, skew):
    ranking = jax.random.permutation(stream_key, amount)
    crowded, common = portions_of(amount, rows * top, reach, skew, True), portions_of(amount, rows * top, reach, skew, False)
    places = jnp.arange(amount)

    def named(lengths, offset_by):
        used = int((lengths > 0).sum())
        fixed = max(1, used // 4)
        shifted = fixed + (places - fixed + offset_by * (used - fixed)) % max(1, amount - fixed)
        return jnp.zeros((amount,), jnp.int32).at[ranking[jnp.where(places < fixed, places, shifted)]].set(jnp.asarray(lengths, jnp.int32))

    lengths = jnp.where(number % 4 == 0, named(crowded, number // 4), named(common, number - number // 4 - 1))
    mixed = jax.random.permutation(jax.random.fold_in(own, 3), amount)
    giver, receiver = mixed[0:amount // 2 * 2:2], mixed[1:amount // 2 * 2:2]
    margin = jnp.minimum(lengths[giver] - 1, reach - lengths[receiver]) // 2
    margin = jnp.where((giver == ranking[0]) | (receiver == ranking[0]) | (lengths[receiver] == 0), 0, jnp.maximum(margin, 0))
    shifted = jax.random.randint(jax.random.fold_in(own, 4), (amount // 2,), 0, 1 << 20) % (margin + 1)
    lengths = lengths.at[giver].add(-shifted).at[receiver].add(shifted)
    members = jnp.searchsorted(jnp.cumsum(lengths), jnp.arange(rows * top), side="right").astype(jnp.int32)
    table = members.reshape(top, rows).T
    table = table[jax.random.permutation(jax.random.fold_in(own, 1), rows)]
    offset_by = jax.random.randint(jax.random.fold_in(own, 2), (rows, 1), 0, top)
    return jnp.take_along_axis(table, (jnp.arange(top)[None, :] + offset_by) % top, axis=1)


def portions_of(count, total, limit, lean, full):
    weights = [(1 << 20) // math.isqrt(standing ** lean) + 1 for standing in range(1, count + 1)]
    largest = limit if full else min(limit, max(-(-total // count), total * weights[0] // sum(weights)))
    least = 1 if total - largest >= count - 1 else 0
    counts, rest = [largest] + [least] * (count - 1), total - largest - least * (count - 1)
    while rest > 0:
        free = [i for i in range(1, count) if counts[i] < largest] or [i for i in range(1, count) if counts[i] < limit]
        mass, remaining = sum([weights[i] for i in free]), rest
        for i in free:
            addition = min(limit - counts[i], max(1, remaining * weights[i] // mass), rest)
            counts[i] = counts[i] + addition
            rest = rest - addition
    return np.array(counts)


def centred(key, shape, width, most, split=(), kind=jnp.bfloat16):
    values = jax.random.normal(key, shape, jnp.float32) * width
    if len(split) > 0:
        values = shard_levels(key, shape, split, -0.22, 0.18) * values
    return jnp.clip(values, min=-most, max=most).astype(kind)


def setup_inputs(seed: int = 0) -> dict:
    splits = jax.random.split(jax.random.key(seed), 5)
    tokens = centred(splits[0], (TOKENS, DW), 1.0, 6.0, ((0, 1024),))
    routes_keys = jax.random.split(jax.random.fold_in(splits[1], 1), TOKENS // TOK)
    routes_turns = jax.random.permutation(jax.random.fold_in(splits[1], 3), TOKENS // TOK)
    routes = jax.vmap(lambda own, number: deal_out(jax.random.fold_in(splits[1], 2), own, number, TOK, EXPERTS, TOPK, CAP, 2))(routes_keys, routes_turns).reshape((TOKENS, TOPK))
    cotangents = centred(splits[2], (TOKENS, TOPK, HID), 1.0, 6.0, ((0, 1024),))
    momentum = centred(splits[3], (DW, EXPERTS * HID), ((TOK * N_DP * TOPK) ** 0.5), 1024.0, ((0, 128), (1, 8)), jnp.float32)
    return {"tokens": tokens, "routes": routes, "cotangents": cotangents, "momentum": momentum}


momentum_decay = 0.95
poly_first = 3.4445
poly_second = -4.775
poly_third = 2.0315
norm_floor = 1e-07
update_gain = 0.2

def orthogonalize(nesterov):
    wide = nesterov.astype(jnp.float32)
    gram = jnp.dot(wide.T, wide, precision=lax.Precision.HIGHEST)
    frobenius = jnp.sqrt(jnp.trace(gram)) + norm_floor
    gram_iter = gram / (frobenius * frobenius)
    iterate = (wide / frobenius).astype(jnp.bfloat16)
    identity = jnp.eye(gram.shape[0], dtype=jnp.float32)
    for section in range(ITERS):
        narrow = gram_iter.astype(jnp.bfloat16)
        squared = jnp.dot(narrow, narrow, preferred_element_type=jnp.float32)
        polynomial = (poly_first * identity + poly_second * gram_iter + poly_third * squared).astype(jnp.bfloat16)
        if section + 1 < ITERS:
            halfway = jnp.dot(narrow, polynomial, preferred_element_type=jnp.float32).astype(jnp.bfloat16)
            gram_iter = jnp.dot(halfway, polynomial, preferred_element_type=jnp.float32)
        product = jnp.dot(iterate, polynomial, preferred_element_type=jnp.float32)
        if section + 1 < ITERS:
            iterate = product.astype(jnp.bfloat16)
        else:
            iterate = product
    return update_gain * math.sqrt(max(DW, HID)) * iterate

def stitch(stacked):
    return jnp.transpose(stacked, (1, 0, 2)).reshape(DW, EXPERTS * HID)

def reference(tokens, routes, cotangents, momentum):
    wide_tokens = tokens.astype(jnp.float32)
    wide_cot = cotangents.astype(jnp.float32)

    def one_expert(expert):
        chosen = (routes == expert).astype(jnp.float32)
        picked = lax.optimization_barrier(jnp.sum(wide_cot * chosen[:, :, None], axis=1))
        gradient = jnp.dot(wide_tokens.T, picked, precision=lax.Precision.HIGHEST)
        old_state = lax.dynamic_slice_in_dim(momentum, (expert * HID).astype(jnp.int32), HID, 1)
        new_state = momentum_decay * old_state + gradient
        nesterov = (gradient + momentum_decay * new_state).astype(jnp.bfloat16)
        return (new_state, orthogonalize(nesterov))
    states, updates = lax.map(one_expert, jnp.arange(EXPERTS, dtype=jnp.int32))
    return (stitch(states), stitch(updates))
```

```python
import math

import jax
import jax.numpy as jnp
from jax import lax
from jax.sharding import Mesh, PartitionSpec as P

ITERS = 2


momentum_decay = 0.95
poly_first = 3.4445
poly_second = -4.775
poly_third = 2.0315
norm_floor = 1e-07
update_gain = 0.2

PLANE = ("z", "x")


def pack(tokens, routes, cotangents, groups, capacity):
    rows, top_count = routes.shape
    pairs = rows * top_count
    pair_routes = routes.reshape(-1)
    member = pair_routes[:, None] == jnp.arange(groups, dtype=jnp.int32)[None, :]
    below = jnp.arange(pairs)[:, None] > jnp.arange(pairs)[None, :]
    earlier = jnp.dot(
        below.astype(jnp.bfloat16),
        member.astype(jnp.bfloat16),
        preferred_element_type=jnp.float32,
    )
    position = jnp.sum(jnp.where(member, earlier, 0.0), axis=1).astype(jnp.int32)
    slot_index = pair_routes * capacity + position
    slots = jnp.arange(groups * capacity, dtype=jnp.int32)
    chosen = (slots[:, None] == slot_index[None, :]).astype(jnp.bfloat16)
    by_token = jnp.sum(chosen.reshape(groups * capacity, rows, top_count), axis=2)
    sent_rows = jnp.dot(by_token, tokens, preferred_element_type=jnp.float32)
    sent_cot = jnp.dot(
        chosen, cotangents.reshape(pairs, -1), preferred_element_type=jnp.float32
    )
    sent = jnp.concatenate(
        [sent_rows.astype(jnp.bfloat16), sent_cot.astype(jnp.bfloat16)], axis=1
    )
    return sent.reshape(groups, capacity, -1)


def body(tokens, routes, cotangents, momentum):
    groups = lax.axis_size("expert")
    cores = lax.axis_size("core")
    chips = lax.axis_size("z") * lax.axis_size("x")
    tok_rows, width = tokens.shape
    hidden = cotangents.shape[2]
    capacity = 2 * tok_rows * routes.shape[1] // groups
    own = width // (chips * cores)
    swap = [(0, 1), (1, 0)]
    core = lax.axis_index("core")

    with jax.named_scope("pack"):
        sent = pack(tokens, routes, cotangents, groups, capacity)
    with jax.named_scope("dispatch"):
        arrived = lax.all_to_all(sent, "expert", split_axis=0, concat_axis=0, tiled=True)
    arrived = arrived.reshape(groups * capacity, width + hidden)
    with jax.named_scope("gradient"):
        partial = lax.dot_general(
            arrived[:, :width],
            arrived[:, width:],
            (((0,), (0,)), ((), ())),
            preferred_element_type=jnp.float32,
        ).reshape(chips, cores, own, hidden)
    with jax.named_scope("reduce"):
        other = lax.dynamic_index_in_dim(partial, 1 - core, 1, keepdims=False)
        mine = lax.dynamic_index_in_dim(partial, core, 1, keepdims=False)
        chip_sum = mine + lax.ppermute(other, "core", swap)
        gradient = jnp.sum(
            lax.all_to_all(chip_sum, PLANE, split_axis=0, concat_axis=0, tiled=True), axis=0
        )
    new_state = momentum_decay * momentum + gradient
    nesterov = (gradient + momentum_decay * new_state).astype(jnp.bfloat16)
    with jax.named_scope("gather"):
        spread = jnp.broadcast_to(nesterov[None], (chips, own, hidden))
        near = lax.all_to_all(spread, PLANE, split_axis=0, concat_axis=0, tiled=True)
        near = near.reshape(chips * own, hidden)
        far = lax.ppermute(near, "core", swap)
    with jax.named_scope("gram"):

        def product(rows):
            return lax.dot_general(
                rows, rows, (((0,), (0,)), ((), ())), preferred_element_type=jnp.float32
            )

        gram = product(near) + product(far)
        total = jnp.sum(jnp.square(near.astype(jnp.float32))) + jnp.sum(
            jnp.square(far.astype(jnp.float32))
        )
    frobenius = jnp.sqrt(total) + norm_floor
    gram_iter = gram / (frobenius * frobenius)
    iterate = (nesterov.astype(jnp.float32) / frobenius).astype(jnp.bfloat16)
    identity = jnp.eye(hidden, dtype=jnp.float32)
    for section in range(ITERS):
        narrow = gram_iter.astype(jnp.bfloat16)
        squared = jnp.dot(narrow, narrow, preferred_element_type=jnp.float32)
        polynomial = (
            poly_first * identity + poly_second * gram_iter + poly_third * squared
        ).astype(jnp.bfloat16)
        if section + 1 < ITERS:
            halfway = jnp.dot(narrow, polynomial, preferred_element_type=jnp.float32).astype(
                jnp.bfloat16
            )
            gram_iter = jnp.dot(halfway, polynomial, preferred_element_type=jnp.float32)
        product_rows = jnp.dot(iterate, polynomial, preferred_element_type=jnp.float32)
        if section + 1 < ITERS:
            iterate = product_rows.astype(jnp.bfloat16)
        else:
            iterate = product_rows
    update = update_gain * math.sqrt(max(width, hidden)) * iterate
    return (new_state, update)


def solution(mesh):
    fine = Mesh(mesh.devices.reshape(8, 8, 2, 8), ("z", "x", "core", "expert"))
    dp = ("z", "x", "core")
    rows = dp + ("expert",)
    in_specs = (P(rows, None), P(rows, None), P(rows, None, None), P(dp, "expert"))
    out_specs = (P(dp, "expert"), P(dp, "expert"))
    return jax.shard_map(body, mesh=fine, in_specs=in_specs, out_specs=out_specs, check_vma=False)
```

```python
import functools
import math

import jax
import jax.numpy as jnp
from jax import lax
from jax.experimental import pallas as pl
from jax.experimental.pallas import tpu as pltpu
from jax.sharding import Mesh, PartitionSpec as P

ITERS = 2


momentum_decay = 0.95
poly_first = 3.4445
poly_second = -4.775
poly_third = 2.0315
norm_floor = 1e-07
update_gain = 0.2

PLANE = ("z", "x")
SWAP = [(0, 1), (1, 0)]
NT = (((1,), (1,)), ((), ()))
TN = (((0,), (0,)), ((), ()))


def pack_kernel(capacity, core_ref, routes_ref, tokens_ref, cot_ref, out_ref):
    top_count, rows = routes_ref.shape
    slots, columns = out_ref.shape
    width = tokens_ref.shape[1]
    groups = slots // capacity
    half = width // 2
    names = lax.broadcasted_iota(jnp.int32, (groups, rows), 0)
    before = (
        lax.broadcasted_iota(jnp.int32, (rows, rows), 0)
        < lax.broadcasted_iota(jnp.int32, (rows, rows), 1)
    ).astype(jnp.bfloat16)
    places = lax.broadcasted_iota(jnp.int32, (slots, rows), 0)
    count = jnp.zeros((groups, 1), jnp.float32)
    chosen = []
    for k in range(top_count):
        route = routes_ref[k:k+1, :]
        member = (names == route).astype(jnp.float32)
        earlier = jnp.dot(member.astype(jnp.bfloat16), before, preferred_element_type=jnp.float32) + count
        position = jnp.sum(earlier * member, axis=0, keepdims=True).astype(jnp.int32)
        count = count + jnp.sum(member, axis=1, keepdims=True)
        chosen.append((places == route * capacity + position).astype(jnp.float32).astype(jnp.bfloat16))
    core = core_ref[0]
    source = lax.broadcasted_iota(jnp.int32, (width, width), 0)
    target = lax.broadcasted_iota(jnp.int32, (width, width), 1)
    within = target % half
    owner = jnp.where(target < half, 1 - core, core)
    wanted = (within // 8) * 16 + owner * 8 + within % 8
    order = (source == wanted).astype(jnp.float32).astype(jnp.bfloat16)
    by_core = jnp.dot(tokens_ref[...], order, preferred_element_type=jnp.float32).astype(jnp.bfloat16)
    by_token = chosen[0]
    for k in range(1, top_count):
        by_token = by_token + chosen[k]
    out_ref[:, :width] = jnp.dot(by_token, by_core, preferred_element_type=jnp.float32).astype(jnp.bfloat16)
    picked = lax.dot_general(chosen[0], cot_ref[0], NT, preferred_element_type=jnp.float32)
    for k in range(1, top_count):
        picked = picked + lax.dot_general(chosen[k], cot_ref[k], NT, preferred_element_type=jnp.float32)
    out_ref[:, width:] = picked.astype(jnp.bfloat16)

def pack(core, routes, tokens, cotangents, groups, capacity):
    rows, width = tokens.shape
    _, top, hidden = cotangents.shape
    slots = groups*capacity
    return pl.pallas_call(
        functools.partial(pack_kernel, capacity),
        out_shape=jax.ShapeDtypeStruct((slots, width+hidden), jnp.bfloat16),
        in_specs=[pl.BlockSpec(memory_space=pltpu.SMEM)]+[pl.BlockSpec(memory_space=pltpu.VMEM)]*3,
        out_specs=pl.BlockSpec(memory_space=pltpu.VMEM),
        compiler_params=pltpu.CompilerParams(vmem_limit_bytes=40*2**20),
        name="pack",
    )(core.reshape(1), routes.T, tokens, jnp.transpose(cotangents,(1,2,0)))

def newton_kernel(iters, gain, near_ref, far_ref, own_ref, out_ref):
    hidden = near_ref.shape[1]
    row = lax.broadcasted_iota(jnp.int32, (hidden, hidden), 0)
    col = lax.broadcasted_iota(jnp.int32, (hidden, hidden), 1)
    diag = row == col
    gram = lax.dot_general(far_ref[...], far_ref[...], TN, preferred_element_type=jnp.float32) + lax.dot_general(near_ref[...], near_ref[...], TN, preferred_element_type=jnp.float32)
    total = jnp.sum(jnp.where(diag, gram, 0.0), keepdims=True)
    frobenius = jnp.sqrt(total) + norm_floor
    gram_iter = gram / (frobenius * frobenius)
    iterate = (own_ref[...].astype(jnp.float32) / frobenius).astype(jnp.bfloat16)
    for section in range(iters):
        narrow = gram_iter.astype(jnp.bfloat16)
        squared = jnp.dot(narrow, narrow, preferred_element_type=jnp.float32)
        polynomial = (jnp.where(diag, poly_first, 0.0) + poly_second * gram_iter + poly_third * squared).astype(jnp.bfloat16)
        product = jnp.dot(iterate, polynomial, preferred_element_type=jnp.float32)
        if section + 1 < iters:
            halfway = jnp.dot(narrow, polynomial, preferred_element_type=jnp.float32).astype(jnp.bfloat16)
            gram_iter = jnp.dot(halfway, polynomial, preferred_element_type=jnp.float32)
            iterate = product.astype(jnp.bfloat16)
    out_ref[...] = gain * product

def newton(near, far, own, iters, gain):
    return pl.pallas_call(
        functools.partial(newton_kernel, iters, gain),
        out_shape=jax.ShapeDtypeStruct(own.shape, jnp.float32),
        in_specs=[pl.BlockSpec(memory_space=pltpu.VMEM)]*3,
        out_specs=pl.BlockSpec(memory_space=pltpu.VMEM),
        compiler_params=pltpu.CompilerParams(vmem_limit_bytes=48*2**20),
        name="newton",
    )(near, far, own)


def body(tokens, routes, cotangents, momentum):
    groups = lax.axis_size("expert")
    cores = lax.axis_size("core")
    chips = lax.axis_size("z") * lax.axis_size("x")
    tok_rows, width = tokens.shape
    hidden = cotangents.shape[2]
    capacity = 2 * tok_rows * routes.shape[1] // groups
    half = width // cores
    own = half // chips
    core = lax.axis_index("core")

    sent = pack(core, routes, tokens, cotangents, groups, capacity)
    with jax.named_scope("dispatch"):
        arrived = lax.all_to_all(
            sent.reshape(groups, capacity, width + hidden),
            "expert",
            split_axis=0,
            concat_axis=0,
            tiled=True,
        ).reshape(groups * capacity, width + hidden)
    with jax.named_scope("gradient"):
        cot = arrived[:, width:]
        other = lax.dot_general(
            arrived[:, :half], cot, TN, preferred_element_type=jnp.float32
        ).reshape(chips, own, hidden)
        swapped = lax.ppermute(other, "core", SWAP)
        mine = lax.dot_general(
            arrived[:, half:width], cot, TN, preferred_element_type=jnp.float32
        ).reshape(chips, own, hidden)
        mine, swapped = lax.optimization_barrier((mine, swapped))
        chip_sum = mine + swapped
    with jax.named_scope("reduce"):
        line_sum = lax.psum_scatter(chip_sum, "z", scatter_dimension=0, tiled=True)
        parts = lax.all_to_all(
            line_sum, "x", split_axis=0, concat_axis=0, tiled=True
        )
        gradient = jnp.sum(parts, axis=0)
    new_state = momentum_decay * momentum + gradient
    nesterov = (gradient + momentum_decay * new_state).astype(jnp.bfloat16)
    with jax.named_scope("gather"):
        spread = jnp.broadcast_to(nesterov[None], (chips, own, hidden))
        near = lax.all_to_all(spread, PLANE, split_axis=0, concat_axis=0, tiled=True)
        far = lax.ppermute(near, "core", SWAP)
    gain = update_gain * math.sqrt(max(width, hidden))
    update = newton(near.reshape(half, hidden), far.reshape(half, hidden), nesterov, ITERS, gain)
    return (new_state, update)


def solution(mesh):
    fine = Mesh(mesh.devices.reshape(8, 8, 2, 8), ("z", "x", "core", "expert"))
    dp = ("z", "x", "core")
    rows = dp + ("expert",)
    in_specs = (P(rows, None), P(rows, None), P(rows, None, None), P(dp, "expert"))
    out_specs = (P(dp, "expert"), P(dp, "expert"))
    return jax.shard_map(body, mesh=fine, in_specs=in_specs, out_specs=out_specs, check_vma=False)
```

```python
import functools
import math

import jax
import jax.numpy as jnp
from jax import lax
from jax.experimental import pallas as pl
from jax.experimental.pallas import tpu as pltpu
from jax.sharding import Mesh, PartitionSpec as P

ITERS = 2


momentum_decay = 0.95
poly_first = 3.4445
poly_second = -4.775
poly_third = 2.0315
norm_floor = 1e-07
update_gain = 0.2

PLANE = ("z", "x")
SWAP = [(0, 1), (1, 0)]
NT = (((1,), (1,)), ((), ()))
TN = (((0,), (0,)), ((), ()))


def pack_kernel(
    capacity, core_ref, routes_hbm, tokens_hbm, cot_hbm, out_ref, routes_ref, tokens_ref, cot_ref, sems
):
    arrivals = [
        pltpu.make_async_copy(source, target, sems.at[number])
        for number, (source, target) in enumerate(
            ((routes_hbm, routes_ref), (tokens_hbm, tokens_ref), (cot_hbm, cot_ref))
        )
    ]
    for arrival in arrivals:
        arrival.start()
    top_count, rows = routes_ref.shape
    slots, columns = out_ref.shape
    width = tokens_ref.shape[1]
    groups = slots // capacity
    half = width // 2
    core = core_ref[0]
    source = lax.broadcasted_iota(jnp.int32, (width, width), 0)
    target = lax.broadcasted_iota(jnp.int32, (width, width), 1)
    within = target % half
    owner = jnp.where(target < half, 1 - core, core)
    wanted = (within // 8) * 16 + owner * 8 + within % 8
    order = (source == wanted).astype(jnp.float32).astype(jnp.bfloat16)
    names = lax.broadcasted_iota(jnp.int32, (groups, rows), 0)
    before = (
        lax.broadcasted_iota(jnp.int32, (rows, rows), 0)
        < lax.broadcasted_iota(jnp.int32, (rows, rows), 1)
    ).astype(jnp.bfloat16)
    places = lax.broadcasted_iota(jnp.int32, (slots, rows), 0)
    count = jnp.zeros((groups, 1), jnp.float32)
    chosen = []
    arrivals[0].wait()
    for k in range(top_count):
        route = routes_ref[k:k+1, :]
        member = (names == route).astype(jnp.float32)
        earlier = jnp.dot(member.astype(jnp.bfloat16), before, preferred_element_type=jnp.float32) + count
        position = jnp.sum(earlier * member, axis=0, keepdims=True).astype(jnp.int32)
        count = count + jnp.sum(member, axis=1, keepdims=True)
        chosen.append((places == route * capacity + position).astype(jnp.float32).astype(jnp.bfloat16))
    arrivals[1].wait()
    by_core = jnp.dot(tokens_ref[...], order, preferred_element_type=jnp.float32).astype(jnp.bfloat16)
    by_token = chosen[0]
    for k in range(1, top_count):
        by_token = by_token + chosen[k]
    out_ref[:, :width] = jnp.dot(by_token, by_core, preferred_element_type=jnp.float32).astype(jnp.bfloat16)
    arrivals[2].wait()
    picked = lax.dot_general(chosen[0], cot_ref[0], NT, preferred_element_type=jnp.float32)
    for k in range(1, top_count):
        picked = picked + lax.dot_general(chosen[k], cot_ref[k], NT, preferred_element_type=jnp.float32)
    out_ref[:, width:] = picked.astype(jnp.bfloat16)

def pack(core, routes, tokens, cotangents, groups, capacity):
    rows, width = tokens.shape
    _, top, hidden = cotangents.shape
    slots = groups*capacity
    return pl.pallas_call(
        functools.partial(pack_kernel, capacity),
        out_shape=jax.ShapeDtypeStruct((slots, width+hidden), jnp.bfloat16),
        in_specs=[pl.BlockSpec(memory_space=pltpu.SMEM)] + [pl.BlockSpec(memory_space=pltpu.HBM)] * 3,
        out_specs=pl.BlockSpec(memory_space=pltpu.VMEM),
        scratch_shapes=[
            pltpu.VMEM((top, rows), jnp.int32),
            pltpu.VMEM((rows, width), jnp.bfloat16),
            pltpu.VMEM((top, hidden, rows), jnp.bfloat16),
            pltpu.SemaphoreType.DMA((3,)),
        ],
        compiler_params=pltpu.CompilerParams(vmem_limit_bytes=40*2**20),
        name="pack",
    )(core.reshape(1), routes.T, tokens, jnp.transpose(cotangents,(1,2,0)))

def newton_kernel(iters, gain, near_ref, far_ref, own_ref, out_ref):
    hidden = near_ref.shape[1]
    row = lax.broadcasted_iota(jnp.int32, (hidden, hidden), 0)
    col = lax.broadcasted_iota(jnp.int32, (hidden, hidden), 1)
    diag = row == col
    gram = near_ref[...] + lax.dot_general(
        far_ref[...], far_ref[...], TN, preferred_element_type=jnp.float32
    )
    total = jnp.sum(jnp.where(diag, gram, 0.0), keepdims=True)
    frobenius = jnp.sqrt(total) + norm_floor
    gram_iter = gram / (frobenius * frobenius)
    iterate = (own_ref[...].astype(jnp.float32) / frobenius).astype(jnp.bfloat16)
    for section in range(iters):
        narrow = gram_iter.astype(jnp.bfloat16)
        squared = jnp.dot(narrow, narrow, preferred_element_type=jnp.float32)
        polynomial = (jnp.where(diag, poly_first, 0.0) + poly_second * gram_iter + poly_third * squared).astype(jnp.bfloat16)
        product = jnp.dot(iterate, polynomial, preferred_element_type=jnp.float32)
        if section + 1 < iters:
            halfway = jnp.dot(narrow, polynomial, preferred_element_type=jnp.float32).astype(jnp.bfloat16)
            gram_iter = jnp.dot(halfway, polynomial, preferred_element_type=jnp.float32)
            iterate = product.astype(jnp.bfloat16)
    out_ref[...] = gain * product

def newton(near, far, own, iters, gain):
    return pl.pallas_call(
        functools.partial(newton_kernel, iters, gain),
        out_shape=jax.ShapeDtypeStruct(own.shape, jnp.float32),
        in_specs=[pl.BlockSpec(memory_space=pltpu.VMEM)]*3,
        out_specs=pl.BlockSpec(memory_space=pltpu.VMEM),
        compiler_params=pltpu.CompilerParams(vmem_limit_bytes=48*2**20),
        name="newton",
    )(near, far, own)


def to_half(values):
    peak = jnp.max(jnp.abs(values))
    power = jnp.clip(jnp.floor(jnp.log2(30000.0 / peak)), -100.0, 100.0)
    scaled = (values * jnp.exp2(power)).astype(jnp.float16)
    free = -values.shape[2] % 128
    tag = jnp.broadcast_to(power.astype(jnp.float16), values.shape[:2] + (free,))
    return jnp.concatenate([scaled, tag], axis=2)


def from_half(parts, hidden):
    scale = jnp.exp2(parts[:, :1, hidden : hidden + 1].astype(jnp.float32))
    return parts[:, :, :hidden].astype(jnp.float32) / scale


def body(tokens, routes, cotangents, momentum):
    groups = lax.axis_size("expert")
    cores = lax.axis_size("core")
    chips = lax.axis_size("z") * lax.axis_size("x")
    tok_rows, width = tokens.shape
    hidden = cotangents.shape[2]
    capacity = 2 * tok_rows * routes.shape[1] // groups
    half = width // cores
    own = half // chips
    core = lax.axis_index("core")

    sent = pack(core, routes, tokens, cotangents, groups, capacity)
    with jax.named_scope("dispatch"):
        arrived = lax.all_to_all(
            sent.reshape(groups, capacity, width + hidden),
            "expert",
            split_axis=0,
            concat_axis=0,
            tiled=True,
        ).reshape(groups * capacity, width + hidden)
    with jax.named_scope("gradient"):
        cot = arrived[:, width:]
        other = lax.dot_general(
            arrived[:, :half], cot, TN, preferred_element_type=jnp.float32
        ).reshape(chips, own, hidden)
        swapped = lax.ppermute(other, "core", SWAP)
        mine = lax.dot_general(
            arrived[:, half:width], cot, TN, preferred_element_type=jnp.float32
        ).reshape(chips, own, hidden)
        mine, swapped = lax.optimization_barrier((mine, swapped))
        chip_sum = mine + swapped
    with jax.named_scope("reduce"):
        sent_sum = to_half(chip_sum)
        parts = lax.all_to_all(sent_sum, PLANE, split_axis=0, concat_axis=0, tiled=True)
        gradient = jnp.sum(from_half(parts, hidden), axis=0)
    new_state = momentum_decay * momentum + gradient
    nesterov = (gradient + momentum_decay * new_state).astype(jnp.bfloat16)
    with jax.named_scope("gather"):
        spread = jnp.broadcast_to(nesterov[None], (chips, own, hidden))
        near = lax.all_to_all(spread, PLANE, split_axis=0, concat_axis=0, tiled=True)
        far = lax.ppermute(near, "core", SWAP).reshape(half, hidden)
        near = near.reshape(half, hidden)
        near_gram = lax.dot_general(near, near, TN, preferred_element_type=jnp.float32)
    gain = update_gain * math.sqrt(max(width, hidden))
    update = newton(near_gram, far, nesterov, ITERS, gain)
    return (new_state, update)


def solution(mesh):
    fine = Mesh(mesh.devices.reshape(8, 8, 2, 8), ("z", "x", "core", "expert"))
    dp = ("z", "x", "core")
    rows = dp + ("expert",)
    in_specs = (P(rows, None), P(rows, None), P(rows, None, None), P(dp, "expert"))
    out_specs = (P(dp, "expert"), P(dp, "expert"))
    return jax.shard_map(body, mesh=fine, in_specs=in_specs, out_specs=out_specs, check_vma=False)
```

```python
import functools
import math

import jax
import jax.numpy as jnp
import numpy as np
from jax import lax
from jax.experimental import pallas as pl
from jax.experimental.pallas import tpu as pltpu
from jax.sharding import Mesh, PartitionSpec as P

ITERS = 2


momentum_decay = 0.95
poly_first = 3.4445
poly_second = -4.775
poly_third = 2.0315
norm_floor = 1e-07
update_gain = 0.2

ALL = ("z", "x", "core", "expert")
X, Y = 1, 2
PLANE = ("z", "x")
SWAP = [(0, 1), (1, 0)]
NT = (((1,), (1,)), ((), ()))
TN = (((0,), (0,)), ((), ()))


def pack_kernel(
    capacity, lines, routes_hbm, tokens_hbm, cot_hbm, out_ref, routes_ref, tokens_ref, cot_ref, sems
):
    arrivals = [
        pltpu.make_async_copy(source, target, sems.at[number])
        for number, (source, target) in enumerate(
            ((routes_hbm, routes_ref), (tokens_hbm, tokens_ref), (cot_hbm, cot_ref))
        )
    ]
    for arrival in arrivals:
        arrival.start()
    top_count, rows = routes_ref.shape
    slots, columns = out_ref.shape
    width = tokens_ref.shape[1]
    groups = slots // capacity
    rest = width // (lines * lines)
    source = lax.broadcasted_iota(jnp.int32, (width, width), 0)
    target = lax.broadcasted_iota(jnp.int32, (width, width), 1)
    first = target // (lines * rest)
    second = target // rest % lines
    wanted = (second * lines + first) * rest + target % rest
    order = (source == wanted).astype(jnp.float32).astype(jnp.bfloat16)
    names = lax.broadcasted_iota(jnp.int32, (groups, rows), 0)
    before = (
        lax.broadcasted_iota(jnp.int32, (rows, rows), 0)
        < lax.broadcasted_iota(jnp.int32, (rows, rows), 1)
    ).astype(jnp.bfloat16)
    places = lax.broadcasted_iota(jnp.int32, (slots, rows), 0)
    count = jnp.zeros((groups, 1), jnp.float32)
    chosen = []
    arrivals[0].wait()
    for k in range(top_count):
        route = routes_ref[k:k+1, :]
        member = (names == route).astype(jnp.float32)
        earlier = jnp.dot(member.astype(jnp.bfloat16), before, preferred_element_type=jnp.float32) + count
        position = jnp.sum(earlier * member, axis=0, keepdims=True).astype(jnp.int32)
        count = count + jnp.sum(member, axis=1, keepdims=True)
        chosen.append((places == route * capacity + position).astype(jnp.float32).astype(jnp.bfloat16))
    arrivals[1].wait()
    by_core = jnp.dot(tokens_ref[...], order, preferred_element_type=jnp.float32).astype(jnp.bfloat16)
    by_token = chosen[0]
    for k in range(1, top_count):
        by_token = by_token + chosen[k]
    out_ref[:, :width] = jnp.dot(by_token, by_core, preferred_element_type=jnp.float32).astype(jnp.bfloat16)
    arrivals[2].wait()
    picked = lax.dot_general(chosen[0], cot_ref[0], NT, preferred_element_type=jnp.float32)
    for k in range(1, top_count):
        picked = picked + lax.dot_general(chosen[k], cot_ref[k], NT, preferred_element_type=jnp.float32)
    out_ref[:, width:] = picked.astype(jnp.bfloat16)

def pack(routes, tokens, cotangents, groups, capacity, lines):
    rows, width = tokens.shape
    _, top, hidden = cotangents.shape
    slots = groups*capacity
    return pl.pallas_call(
        functools.partial(pack_kernel, capacity, lines),
        out_shape=jax.ShapeDtypeStruct((slots, width+hidden), jnp.bfloat16),
        in_specs=[pl.BlockSpec(memory_space=pl.ANY)] * 3,
        out_specs=pl.BlockSpec(memory_space=pltpu.VMEM),
        scratch_shapes=[
            pltpu.VMEM((top, rows), jnp.int32),
            pltpu.VMEM((rows, width), jnp.bfloat16),
            pltpu.VMEM((top, hidden, rows), jnp.bfloat16),
            pltpu.SemaphoreType.DMA((3,)),
        ],
        compiler_params=pltpu.CompilerParams(vmem_limit_bytes=60 * 2**20),
        name="pack",
    )(routes.T, tokens, jnp.transpose(cotangents,(1,2,0)))

def newton_kernel(iters, gain, near_ref, far_ref, own_ref, out_ref):
    hidden = near_ref.shape[1]
    row = lax.broadcasted_iota(jnp.int32, (hidden, hidden), 0)
    col = lax.broadcasted_iota(jnp.int32, (hidden, hidden), 1)
    diag = row == col
    gram = near_ref[...] + lax.dot_general(
        far_ref[...], far_ref[...], TN, preferred_element_type=jnp.float32
    )
    total = jnp.sum(jnp.where(diag, gram, 0.0), keepdims=True)
    frobenius = jnp.sqrt(total) + norm_floor
    gram_iter = gram / (frobenius * frobenius)
    iterate = (own_ref[...].astype(jnp.float32) / frobenius).astype(jnp.bfloat16)
    for section in range(iters):
        narrow = gram_iter.astype(jnp.bfloat16)
        squared = jnp.dot(narrow, narrow, preferred_element_type=jnp.float32)
        polynomial = (jnp.where(diag, poly_first, 0.0) + poly_second * gram_iter + poly_third * squared).astype(jnp.bfloat16)
        product = jnp.dot(iterate, polynomial, preferred_element_type=jnp.float32)
        if section + 1 < iters:
            halfway = jnp.dot(narrow, polynomial, preferred_element_type=jnp.float32).astype(jnp.bfloat16)
            gram_iter = jnp.dot(halfway, polynomial, preferred_element_type=jnp.float32)
            iterate = product.astype(jnp.bfloat16)
    out_ref[...] = gain * product

def newton(near, far, own, iters, gain):
    return pl.pallas_call(
        functools.partial(newton_kernel, iters, gain),
        out_shape=jax.ShapeDtypeStruct(own.shape, jnp.float32),
        in_specs=[pl.BlockSpec(memory_space=pltpu.VMEM)]*3,
        out_specs=pl.BlockSpec(memory_space=pltpu.VMEM),
        compiler_params=pltpu.CompilerParams(vmem_limit_bytes=48*2**20),
        name="newton",
    )(near, far, own)


def to_half(values):
    peak = jnp.max(jnp.abs(values))
    power = jnp.clip(jnp.floor(jnp.log2(30000.0 / peak)), -100.0, 100.0)
    scaled = (values * jnp.exp2(power)).astype(jnp.float16)
    tag = jnp.broadcast_to(power.astype(jnp.float16), values.shape[:2] + (16,))
    return jnp.concatenate([scaled, tag], axis=2)


def from_half(parts, hidden):
    scale = jnp.exp2(parts[:, :, hidden : hidden + 1].astype(jnp.float32))
    return parts[:, :, :hidden].astype(jnp.float32) / scale


def placed(sizes, along):
    grid = np.arange(math.prod(sizes)).reshape(sizes)
    groups = []
    for core, axis in enumerate(along):
        part = np.moveaxis(grid[:, :, core, :], axis, -1)
        groups += part.reshape(-1, part.shape[-1]).tolist()
    return groups


def exchange(values, along):
    sizes = tuple(lax.axis_size(name) for name in ALL)
    return lax.all_to_all(
        values,
        ALL,
        split_axis=0,
        concat_axis=0,
        axis_index_groups=placed(sizes, along),
        tiled=True,
    )


def meet(rows):
    z, x, cores, y = (lax.axis_size(name) for name in ALL)
    own = rows.shape[0] // cores
    grid = np.arange(z * x * cores * y).reshape(z, x, cores, y)
    turned = np.transpose(grid, (0, 3, 2, 1))
    low = list(zip(grid[:, :, 0].ravel().tolist(), grid[:, :, 1].ravel().tolist()))
    low += list(zip(grid[:, :, 1].ravel().tolist(), turned[:, :, 0].ravel().tolist()))
    high = list(zip(grid[:, :, 1].ravel().tolist(), turned[:, :, 1].ravel().tolist()))
    zero = lax.axis_index("core") == 0
    crossing = lax.ppermute(jnp.where(zero, rows[own:], rows[:own]), ALL, low)
    across = lax.ppermute(rows[own:], ALL, high)
    return crossing + jnp.where(zero, rows[:own], across)


def body(tokens, routes, cotangents, momentum):
    groups = lax.axis_size("expert")
    cores = lax.axis_size("core")
    lines = lax.axis_size("x")
    chips = lax.axis_size("z") * lines
    tok_rows, width = tokens.shape
    hidden = cotangents.shape[2]
    capacity = 2 * tok_rows * routes.shape[1] // groups
    half = width // cores
    own = half // chips

    sent = pack(routes, tokens, cotangents, groups, capacity, lines)
    with jax.named_scope("dispatch"):
        arrived = exchange(sent.reshape(groups, capacity, width + hidden), (Y, X))
        arrived = arrived.reshape(groups * capacity, width + hidden)
    with jax.named_scope("gradient"):
        partial = lax.dot_general(
            arrived[:, :width], arrived[:, width:], TN, preferred_element_type=jnp.float32
        ).reshape(lines, width // lines, hidden)
    with jax.named_scope("reduce"):
        parts = exchange(to_half(partial), (X, Y))
        line_sum = jnp.sum(from_half(parts, hidden), axis=0)
        parts = lax.all_to_all(
            line_sum.reshape(-1, cores * own, hidden), "z", split_axis=0, concat_axis=0, tiled=True
        )
        gradient = meet(jnp.sum(parts, axis=0))
    new_state = momentum_decay * momentum + gradient
    nesterov = (gradient + momentum_decay * new_state).astype(jnp.bfloat16)
    with jax.named_scope("gather"):
        spread = jnp.broadcast_to(nesterov[None], (chips, own, hidden))
        near = lax.all_to_all(spread, PLANE, split_axis=0, concat_axis=0, tiled=True)
        far = lax.ppermute(near, "core", SWAP).reshape(half, hidden)
        near = near.reshape(half, hidden)
        near_gram = lax.dot_general(near, near, TN, preferred_element_type=jnp.float32)
    gain = update_gain * math.sqrt(max(width, hidden))
    update = newton(near_gram, far, nesterov, ITERS, gain)
    return (new_state, update)


def solution(mesh):
    lines = mesh.devices.shape[1]
    fine = Mesh(mesh.devices.reshape(lines, lines, -1, lines), ALL)
    dp = ALL[:3]
    rows = ALL
    in_specs = (P(rows, None), P(rows, None), P(rows, None, None), P(dp, "expert"))
    out_specs = (P(dp, "expert"), P(dp, "expert"))
    return jax.shard_map(body, mesh=fine, in_specs=in_specs, out_specs=out_specs, check_vma=False)
```

```python
import functools
import math

import jax
import jax.numpy as jnp
from jax import lax
from jax.experimental import pallas as pl
from jax.experimental.pallas import tpu as pltpu
from jax.sharding import Mesh, PartitionSpec as P

ITERS = 2


momentum_decay = 0.95
poly_first = 3.4445
poly_second = -4.775
poly_third = 2.0315
norm_floor = 1e-07
update_gain = 0.2

PLANE = ("z", "x")
DP = ("z", "x", "core")
SWAP = [(0, 1), (1, 0)]
NT = (((1,), (1,)), ((), ()))
TN = (((0,), (0,)), ((), ()))


def pack_kernel(
    capacity, core_ref, routes_hbm, tokens_hbm, cot_hbm, out_ref, routes_ref, tokens_ref, cot_ref, sems
):
    arrivals = [
        pltpu.make_async_copy(source, target, sems.at[number])
        for number, (source, target) in enumerate(
            ((routes_hbm, routes_ref), (tokens_hbm, tokens_ref), (cot_hbm, cot_ref))
        )
    ]
    for arrival in arrivals:
        arrival.start()
    top_count, rows = routes_ref.shape
    slots, columns = out_ref.shape
    width = tokens_ref.shape[1]
    groups = slots // capacity
    half = width // 2
    core = core_ref[0]
    source = lax.broadcasted_iota(jnp.int32, (width, width), 0)
    target = lax.broadcasted_iota(jnp.int32, (width, width), 1)
    within = target % half
    owner = jnp.where(target < half, 1 - core, core)
    wanted = (within // 8) * 16 + owner * 8 + within % 8
    order = (source == wanted).astype(jnp.float32).astype(jnp.bfloat16)
    names = lax.broadcasted_iota(jnp.int32, (groups, rows), 0)
    before = (
        lax.broadcasted_iota(jnp.int32, (rows, rows), 0)
        < lax.broadcasted_iota(jnp.int32, (rows, rows), 1)
    ).astype(jnp.bfloat16)
    places = lax.broadcasted_iota(jnp.int32, (slots, rows), 0)
    count = jnp.zeros((groups, 1), jnp.float32)
    chosen = []
    arrivals[0].wait()
    for k in range(top_count):
        route = routes_ref[k:k+1, :]
        member = (names == route).astype(jnp.float32)
        earlier = jnp.dot(member.astype(jnp.bfloat16), before, preferred_element_type=jnp.float32) + count
        position = jnp.sum(earlier * member, axis=0, keepdims=True).astype(jnp.int32)
        count = count + jnp.sum(member, axis=1, keepdims=True)
        chosen.append((places == route * capacity + position).astype(jnp.float32).astype(jnp.bfloat16))
    arrivals[1].wait()
    by_core = jnp.dot(tokens_ref[...], order, preferred_element_type=jnp.float32).astype(jnp.bfloat16)
    by_token = chosen[0]
    for k in range(1, top_count):
        by_token = by_token + chosen[k]
    out_ref[:, :width] = jnp.dot(by_token, by_core, preferred_element_type=jnp.float32).astype(jnp.bfloat16)
    arrivals[2].wait()
    picked = lax.dot_general(chosen[0], cot_ref[0], NT, preferred_element_type=jnp.float32)
    for k in range(1, top_count):
        picked = picked + lax.dot_general(chosen[k], cot_ref[k], NT, preferred_element_type=jnp.float32)
    out_ref[:, width:] = picked.astype(jnp.bfloat16)

def pack(core, routes, tokens, cotangents, groups, capacity):
    rows, width = tokens.shape
    _, top, hidden = cotangents.shape
    slots = groups*capacity
    return pl.pallas_call(
        functools.partial(pack_kernel, capacity),
        out_shape=jax.ShapeDtypeStruct((slots, width+hidden), jnp.bfloat16),
        in_specs=[pl.BlockSpec(memory_space=pltpu.SMEM)] + [pl.BlockSpec(memory_space=pl.ANY)] * 3,
        out_specs=pl.BlockSpec(memory_space=pltpu.VMEM),
        scratch_shapes=[
            pltpu.VMEM((top, rows), jnp.int32),
            pltpu.VMEM((rows, width), jnp.bfloat16),
            pltpu.VMEM((top, hidden, rows), jnp.bfloat16),
            pltpu.SemaphoreType.DMA((3,)),
        ],
        compiler_params=pltpu.CompilerParams(vmem_limit_bytes=60 * 2**20),
        name="pack",
    )(core.reshape(1), routes.T, tokens, jnp.transpose(cotangents,(1,2,0)))

def newton_kernel(iters, gain, every_ref, own_ref, out_ref):
    hidden = every_ref.shape[1]
    row = lax.broadcasted_iota(jnp.int32, (hidden, hidden), 0)
    col = lax.broadcasted_iota(jnp.int32, (hidden, hidden), 1)
    diag = row == col
    gram = lax.dot_general(
        every_ref[...], every_ref[...], TN, preferred_element_type=jnp.float32
    )
    total = jnp.sum(jnp.where(diag, gram, 0.0), keepdims=True)
    frobenius = jnp.sqrt(total) + norm_floor
    gram_iter = gram / (frobenius * frobenius)
    iterate = (own_ref[...].astype(jnp.float32) / frobenius).astype(jnp.bfloat16)
    for section in range(iters):
        narrow = gram_iter.astype(jnp.bfloat16)
        squared = jnp.dot(narrow, narrow, preferred_element_type=jnp.float32)
        polynomial = (jnp.where(diag, poly_first, 0.0) + poly_second * gram_iter + poly_third * squared).astype(jnp.bfloat16)
        product = jnp.dot(iterate, polynomial, preferred_element_type=jnp.float32)
        if section + 1 < iters:
            halfway = jnp.dot(narrow, polynomial, preferred_element_type=jnp.float32).astype(jnp.bfloat16)
            gram_iter = jnp.dot(halfway, polynomial, preferred_element_type=jnp.float32)
            iterate = product.astype(jnp.bfloat16)
    out_ref[...] = gain * product

def newton(every, own, iters, gain):
    return pl.pallas_call(
        functools.partial(newton_kernel, iters, gain),
        out_shape=jax.ShapeDtypeStruct(own.shape, jnp.float32),
        in_specs=[pl.BlockSpec(memory_space=pltpu.VMEM)] * 2,
        out_specs=pl.BlockSpec(memory_space=pltpu.VMEM),
        compiler_params=pltpu.CompilerParams(vmem_limit_bytes=48 * 2**20),
        name="newton",
    )(every, own)


def to_half(values):
    peak = jnp.max(jnp.abs(values))
    power = jnp.clip(jnp.floor(jnp.log2(30000.0 / peak)), -100.0, 100.0)
    scaled = (values * jnp.exp2(power)).astype(jnp.float16)
    free = -values.shape[2] % 128
    tag = jnp.broadcast_to(power.astype(jnp.float16), values.shape[:2] + (free,))
    return jnp.concatenate([scaled, tag], axis=2)


def from_half(parts, hidden):
    scale = jnp.exp2(parts[:, :, hidden : hidden + 1].astype(jnp.float32))
    return parts[:, :, :hidden].astype(jnp.float32) / scale


def body(tokens, routes, cotangents, momentum):
    groups = lax.axis_size("expert")
    cores = lax.axis_size("core")
    chips = lax.axis_size("z") * lax.axis_size("x")
    tok_rows, width = tokens.shape
    hidden = cotangents.shape[2]
    capacity = 2 * tok_rows * routes.shape[1] // groups
    half = width // cores
    own = half // chips
    core = lax.axis_index("core")

    sent = pack(core, routes, tokens, cotangents, groups, capacity)
    with jax.named_scope("dispatch"):
        arrived = lax.all_to_all(
            sent.reshape(groups, capacity, width + hidden),
            "expert",
            split_axis=0,
            concat_axis=0,
            tiled=True,
        ).reshape(groups * capacity, width + hidden)
    with jax.named_scope("gradient"):
        cot = arrived[:, width:]
        other = lax.dot_general(
            arrived[:, :half], cot, TN, preferred_element_type=jnp.float32
        ).reshape(chips, own, hidden)
        swapped = lax.ppermute(other, "core", SWAP)
        mine = lax.dot_general(
            arrived[:, half:width], cot, TN, preferred_element_type=jnp.float32
        ).reshape(chips, own, hidden)
        mine, swapped = lax.optimization_barrier((mine, swapped))
        chip_sum = mine + swapped
    with jax.named_scope("reduce"):
        sent_sum = to_half(chip_sum)
        parts = lax.all_to_all(sent_sum, PLANE, split_axis=0, concat_axis=0, tiled=True)
        gradient = jnp.sum(from_half(parts, hidden), axis=0)
    new_state = momentum_decay * momentum + gradient
    nesterov = (gradient + momentum_decay * new_state).astype(jnp.bfloat16)
    with jax.named_scope("gather"):
        every = lax.all_gather(nesterov, DP, axis=0, tiled=True)
    gain = update_gain * math.sqrt(max(width, hidden))
    update = newton(every, nesterov, ITERS, gain)
    return (new_state, update)


def solution(mesh):
    fine = Mesh(mesh.devices.reshape(8, 8, 2, 8), ("z", "x", "core", "expert"))
    dp = DP
    rows = dp + ("expert",)
    in_specs = (P(rows, None), P(rows, None), P(rows, None, None), P(dp, "expert"))
    out_specs = (P(dp, "expert"), P(dp, "expert"))
    return jax.shard_map(body, mesh=fine, in_specs=in_specs, out_specs=out_specs, check_vma=False)
```

```python
import functools
import math

import jax
import jax.numpy as jnp
import numpy as np
from jax import lax
from jax.experimental import pallas as pl
from jax.experimental.pallas import tpu as pltpu
from jax.sharding import Mesh, PartitionSpec as P

ITERS = 2


momentum_decay = 0.95
poly_first = 3.4445
poly_second = -4.775
poly_third = 2.0315
norm_floor = 1e-07
update_gain = 0.2

ALL = ("z", "x", "core", "expert")
Z, X, Y = 0, 1, 2
PLANE = ("z", "x")
SWAP = [(0, 1), (1, 0)]
NT = (((1,), (1,)), ((), ()))
TN = (((0,), (0,)), ((), ()))


def pack_kernel(
    capacity, lines, core_ref, routes_hbm, tokens_hbm, cot_hbm, out_ref, routes_ref, tokens_ref, cot_ref, sems
):
    arrivals = [
        pltpu.make_async_copy(source, target, sems.at[number])
        for number, (source, target) in enumerate(
            ((routes_hbm, routes_ref), (tokens_hbm, tokens_ref), (cot_hbm, cot_ref))
        )
    ]
    for arrival in arrivals:
        arrival.start()
    top_count, rows = routes_ref.shape
    slots, columns = out_ref.shape
    width = tokens_ref.shape[1]
    groups = slots // capacity
    rest = width // (lines * lines)
    source = lax.broadcasted_iota(jnp.int32, (width, width), 0)
    target = lax.broadcasted_iota(jnp.int32, (width, width), 1)
    first = target // (lines * rest)
    second = target // rest % lines
    place = jnp.where(core_ref[0] == 0, second * lines + first, first * lines + second)
    wanted = place * rest + target % rest
    order = (source == wanted).astype(jnp.float32).astype(jnp.bfloat16)
    names = lax.broadcasted_iota(jnp.int32, (groups, rows), 0)
    before = (
        lax.broadcasted_iota(jnp.int32, (rows, rows), 0)
        < lax.broadcasted_iota(jnp.int32, (rows, rows), 1)
    ).astype(jnp.bfloat16)
    places = lax.broadcasted_iota(jnp.int32, (slots, rows), 0)
    count = jnp.zeros((groups, 1), jnp.float32)
    chosen = []
    arrivals[0].wait()
    for k in range(top_count):
        route = routes_ref[k:k+1, :]
        member = (names == route).astype(jnp.float32)
        earlier = jnp.dot(member.astype(jnp.bfloat16), before, preferred_element_type=jnp.float32) + count
        position = jnp.sum(earlier * member, axis=0, keepdims=True).astype(jnp.int32)
        count = count + jnp.sum(member, axis=1, keepdims=True)
        chosen.append((places == route * capacity + position).astype(jnp.float32).astype(jnp.bfloat16))
    arrivals[1].wait()
    by_core = jnp.dot(tokens_ref[...], order, preferred_element_type=jnp.float32).astype(jnp.bfloat16)
    by_token = chosen[0]
    for k in range(1, top_count):
        by_token = by_token + chosen[k]
    out_ref[:, :width] = jnp.dot(by_token, by_core, preferred_element_type=jnp.float32).astype(jnp.bfloat16)
    arrivals[2].wait()
    picked = lax.dot_general(chosen[0], cot_ref[0], NT, preferred_element_type=jnp.float32)
    for k in range(1, top_count):
        picked = picked + lax.dot_general(chosen[k], cot_ref[k], NT, preferred_element_type=jnp.float32)
    out_ref[:, width:] = picked.astype(jnp.bfloat16)

def pack(core, routes, tokens, cotangents, groups, capacity, lines):
    rows, width = tokens.shape
    _, top, hidden = cotangents.shape
    slots = groups*capacity
    return pl.pallas_call(
        functools.partial(pack_kernel, capacity, lines),
        out_shape=jax.ShapeDtypeStruct((slots, width+hidden), jnp.bfloat16),
        in_specs=[pl.BlockSpec(memory_space=pltpu.SMEM)] + [pl.BlockSpec(memory_space=pl.ANY)] * 3,
        out_specs=pl.BlockSpec(memory_space=pltpu.VMEM),
        scratch_shapes=[
            pltpu.VMEM((top, rows), jnp.int32),
            pltpu.VMEM((rows, width), jnp.bfloat16),
            pltpu.VMEM((top, hidden, rows), jnp.bfloat16),
            pltpu.SemaphoreType.DMA((3,)),
        ],
        compiler_params=pltpu.CompilerParams(vmem_limit_bytes=60 * 2**20),
        name="pack",
    )(core.reshape(1), routes.T, tokens, jnp.transpose(cotangents,(1,2,0)))

def newton_kernel(iters, gain, near_ref, far_ref, own_ref, out_ref):
    hidden = near_ref.shape[1]
    row = lax.broadcasted_iota(jnp.int32, (hidden, hidden), 0)
    col = lax.broadcasted_iota(jnp.int32, (hidden, hidden), 1)
    diag = row == col
    gram = near_ref[...] + lax.dot_general(
        far_ref[...], far_ref[...], TN, preferred_element_type=jnp.float32
    )
    total = jnp.sum(jnp.where(diag, gram, 0.0), keepdims=True)
    frobenius = jnp.sqrt(total) + norm_floor
    gram_iter = gram / (frobenius * frobenius)
    iterate = (own_ref[...].astype(jnp.float32) / frobenius).astype(jnp.bfloat16)
    for section in range(iters):
        narrow = gram_iter.astype(jnp.bfloat16)
        squared = jnp.dot(narrow, narrow, preferred_element_type=jnp.float32)
        polynomial = (jnp.where(diag, poly_first, 0.0) + poly_second * gram_iter + poly_third * squared).astype(jnp.bfloat16)
        product = jnp.dot(iterate, polynomial, preferred_element_type=jnp.float32)
        if section + 1 < iters:
            halfway = jnp.dot(narrow, polynomial, preferred_element_type=jnp.float32).astype(jnp.bfloat16)
            gram_iter = jnp.dot(halfway, polynomial, preferred_element_type=jnp.float32)
            iterate = product.astype(jnp.bfloat16)
    out_ref[...] = gain * product

def newton(near, far, own, iters, gain):
    return pl.pallas_call(
        functools.partial(newton_kernel, iters, gain),
        out_shape=jax.ShapeDtypeStruct(own.shape, jnp.float32),
        in_specs=[pl.BlockSpec(memory_space=pltpu.VMEM)]*3,
        out_specs=pl.BlockSpec(memory_space=pltpu.VMEM),
        compiler_params=pltpu.CompilerParams(vmem_limit_bytes=48*2**20),
        name="newton",
    )(near, far, own)


def to_half(values):
    peak = jnp.max(jnp.abs(values))
    power = jnp.clip(jnp.floor(jnp.log2(30000.0 / peak)), -100.0, 100.0)
    scaled = (values * jnp.exp2(power)).astype(jnp.float16)
    tag = jnp.broadcast_to(power.astype(jnp.float16), values.shape[:2] + (16,))
    return jnp.concatenate([scaled, tag], axis=2)


def from_half(parts, hidden):
    scale = jnp.exp2(parts[:, :, hidden : hidden + 1].astype(jnp.float32))
    return parts[:, :, :hidden].astype(jnp.float32) / scale


def placed(sizes, along):
    grid = np.arange(math.prod(sizes)).reshape(sizes)
    groups = []
    for core, axis in enumerate(along):
        part = np.moveaxis(grid[:, :, core, :], axis, -1)
        groups += part.reshape(-1, part.shape[-1]).tolist()
    return groups


def exchange(values, along):
    sizes = tuple(lax.axis_size(name) for name in ALL)
    return lax.all_to_all(
        values,
        ALL,
        split_axis=0,
        concat_axis=0,
        axis_index_groups=placed(sizes, along),
        tiled=True,
    )


def meet(rows):
    z, x, cores, y = (lax.axis_size(name) for name in ALL)
    own = rows.shape[0] // cores
    grid = np.arange(z * x * cores * y).reshape(z, x, cores, y)
    turned = np.transpose(grid, (3, 1, 2, 0))
    low = list(zip(grid[:, :, 0].ravel().tolist(), grid[:, :, 1].ravel().tolist()))
    low += list(zip(grid[:, :, 1].ravel().tolist(), turned[:, :, 0].ravel().tolist()))
    high = list(zip(grid[:, :, 1].ravel().tolist(), turned[:, :, 1].ravel().tolist()))
    zero = lax.axis_index("core") == 0
    crossing = lax.ppermute(jnp.where(zero, rows[own:], rows[:own]), ALL, low)
    across = lax.ppermute(rows[own:], ALL, high)
    return crossing + jnp.where(zero, rows[:own], across)


def body(tokens, routes, cotangents, momentum):
    groups = lax.axis_size("expert")
    cores = lax.axis_size("core")
    lines = lax.axis_size("x")
    chips = lax.axis_size("z") * lines
    tok_rows, width = tokens.shape
    hidden = cotangents.shape[2]
    capacity = 2 * tok_rows * routes.shape[1] // groups
    half = width // cores
    own = half // chips

    sent = pack(lax.axis_index("core"), routes, tokens, cotangents, groups, capacity, lines)
    with jax.named_scope("dispatch"):
        arrived = exchange(sent.reshape(groups, capacity, width + hidden), (Y, Z))
        arrived = arrived.reshape(groups * capacity, width + hidden)
    with jax.named_scope("gradient"):
        partial = lax.dot_general(
            arrived[:, :width], arrived[:, width:], TN, preferred_element_type=jnp.float32
        ).reshape(lines, width // lines, hidden)
    with jax.named_scope("reduce"):
        parts = exchange(to_half(partial), (X, Y))
        line_sum = jnp.sum(from_half(parts, hidden), axis=0)
        parts = exchange(line_sum.reshape(-1, cores * own, hidden), (Z, X))
        gradient = meet(jnp.sum(parts, axis=0))
    new_state = momentum_decay * momentum + gradient
    nesterov = (gradient + momentum_decay * new_state).astype(jnp.bfloat16)
    with jax.named_scope("gather"):
        spread = jnp.broadcast_to(nesterov[None], (chips, own, hidden))
        near = lax.all_to_all(spread, PLANE, split_axis=0, concat_axis=0, tiled=True)
        far = lax.ppermute(near, "core", SWAP).reshape(half, hidden)
        near = near.reshape(half, hidden)
        near_gram = lax.dot_general(near, near, TN, preferred_element_type=jnp.float32)
    gain = update_gain * math.sqrt(max(width, hidden))
    update = newton(near_gram, far, nesterov, ITERS, gain)
    return (new_state, update)


def solution(mesh):
    lines = mesh.devices.shape[1]
    fine = Mesh(mesh.devices.reshape(lines, lines, -1, lines), ALL)
    dp = ALL[:3]
    rows = ALL
    in_specs = (P(rows, None), P(rows, None), P(rows, None, None), P(dp, "expert"))
    out_specs = (P(dp, "expert"), P(dp, "expert"))
    return jax.shard_map(body, mesh=fine, in_specs=in_specs, out_specs=out_specs, check_vma=False)
```

```python
import functools
import math

import jax
import jax.numpy as jnp
import numpy as np
from jax import lax
from jax.experimental import pallas as pl
from jax.experimental.pallas import tpu as pltpu
from jax.sharding import Mesh, PartitionSpec as P

ITERS = 2


momentum_decay = 0.95
poly_first = 3.4445
poly_second = -4.775
poly_third = 2.0315
norm_floor = 1e-07
update_gain = 0.2

ALL = ("z", "x", "core", "expert")
Z, X, Y = 0, 1, 2
PLANE = ("z", "x")
SWAP = [(0, 1), (1, 0)]
LANES = 128
TAG = 16
NT = (((1,), (1,)), ((), ()))
TN = (((0,), (0,)), ((), ()))


def pack_kernel(
    capacity, lines, core_ref, routes_hbm, tokens_hbm, cot_hbm, out_hbm, routes_ref, tokens_ref, cot_ref, out_ref, sems
):
    arrivals = [
        pltpu.make_async_copy(source, target, sems.at[number])
        for number, (source, target) in enumerate(
            ((routes_hbm, routes_ref), (tokens_hbm, tokens_ref), (cot_hbm, cot_ref))
        )
    ]
    for arrival in arrivals:
        arrival.start()
    top_count, rows = routes_ref.shape
    groups = out_ref.shape[0]
    slots = groups * capacity
    width = tokens_ref.shape[1]
    rest = width // (lines * lines)
    source = lax.broadcasted_iota(jnp.int32, (width, width), 0)
    target = lax.broadcasted_iota(jnp.int32, (width, width), 1)
    first = target // (lines * rest)
    second = target // rest % lines
    place = jnp.where(core_ref[0] == 0, second * lines + first, first * lines + second)
    wanted = place * rest + target % rest
    order = (source == wanted).astype(jnp.float32).astype(jnp.bfloat16)
    names = lax.broadcasted_iota(jnp.int32, (groups, rows), 0)
    before = (
        lax.broadcasted_iota(jnp.int32, (rows, rows), 0)
        < lax.broadcasted_iota(jnp.int32, (rows, rows), 1)
    ).astype(jnp.bfloat16)
    places = lax.broadcasted_iota(jnp.int32, (slots, rows), 0)
    count = jnp.zeros((groups, 1), jnp.float32)
    chosen = []
    arrivals[0].wait()
    for k in range(top_count):
        route = routes_ref[k:k+1, :]
        member = (names == route).astype(jnp.float32)
        earlier = jnp.dot(member.astype(jnp.bfloat16), before, preferred_element_type=jnp.float32) + count
        position = jnp.sum(earlier * member, axis=0, keepdims=True).astype(jnp.int32)
        count = count + jnp.sum(member, axis=1, keepdims=True)
        chosen.append((places == route * capacity + position).astype(jnp.float32).astype(jnp.bfloat16))
    arrivals[2].wait()
    picked = lax.dot_general(chosen[0], cot_ref[0], NT, preferred_element_type=jnp.float32)
    for k in range(1, top_count):
        picked = picked + lax.dot_general(
            chosen[k], cot_ref[k], NT, preferred_element_type=jnp.float32
        )
    picked = picked.astype(jnp.bfloat16)
    hidden = picked.shape[1]
    start = width // LANES * capacity
    for tile in range(hidden // LANES):
        part = picked[:, tile * LANES : (tile + 1) * LANES].reshape(groups, capacity, LANES)
        out_ref[:, start : start + capacity, :] = part
        start += capacity
    rest_columns = hidden % LANES
    if rest_columns:
        part = picked[:, hidden - rest_columns :].reshape(groups, capacity, rest_columns)
        out_ref[:, start:, :] = jnp.concatenate(
            [part[:, : capacity // 2], part[:, capacity // 2 :]], axis=2
        )

    def leave(begin, end, number):
        departure = pltpu.make_async_copy(
            out_ref.at[:, begin:end, :], out_hbm.at[:, begin:end, :], sems.at[number]
        )
        departure.start()
        return departure

    first = width // LANES * capacity
    departures = [leave(first, out_ref.shape[1], 3)]
    arrivals[1].wait()
    by_core = jnp.dot(
        tokens_ref[...], order, preferred_element_type=jnp.float32
    ).astype(jnp.bfloat16)
    by_token = chosen[0]
    for k in range(1, top_count):
        by_token = by_token + chosen[k]
    middle = width // 2
    for side in range(2):
        sent = jnp.dot(
            by_token,
            by_core[:, side * middle : (side + 1) * middle],
            preferred_element_type=jnp.float32,
        ).astype(jnp.bfloat16)
        for tile in range(middle // LANES):
            begin = side * first // 2 + tile * capacity
            part = sent[:, tile * LANES : (tile + 1) * LANES].reshape(groups, capacity, LANES)
            out_ref[:, begin : begin + capacity, :] = part
        departures.append(leave(side * first // 2, (side + 1) * first // 2, 4 + side))
    for departure in departures:
        departure.wait()


def pack(core, routes, tokens, cotangents, groups, capacity, lines):
    rows, width = tokens.shape
    _, top, hidden = cotangents.shape
    filled = capacity * (width + hidden) // LANES
    return pl.pallas_call(
        functools.partial(pack_kernel, capacity, lines),
        out_shape=jax.ShapeDtypeStruct((groups, filled, LANES), jnp.bfloat16),
        in_specs=[pl.BlockSpec(memory_space=pltpu.SMEM)] + [pl.BlockSpec(memory_space=pl.ANY)] * 3,
        out_specs=pl.BlockSpec(memory_space=pl.ANY),
        scratch_shapes=[
            pltpu.VMEM((top, rows), jnp.int32),
            pltpu.VMEM((rows, width), jnp.bfloat16),
            pltpu.VMEM((top, hidden, rows), jnp.bfloat16),
            pltpu.VMEM((groups, filled, LANES), jnp.bfloat16),
            pltpu.SemaphoreType.DMA((6,)),
        ],
        compiler_params=pltpu.CompilerParams(vmem_limit_bytes=60 * 2**20),
        name="pack",
    )(core.reshape(1), routes.T, tokens, jnp.transpose(cotangents,(1,2,0)))

def gradient_kernel(width, hidden, arrived_ref, out_ref):
    groups, filled, _ = arrived_ref.shape
    capacity = filled * LANES // (width + hidden)
    slots = groups * capacity

    def tile(number):
        part = arrived_ref[:, number * capacity : (number + 1) * capacity, :]
        return part.reshape(slots, LANES)

    first = width // LANES
    whole = filled // capacity
    pieces = [tile(number) for number in range(first, whole)]
    if filled % capacity:
        last = arrived_ref[:, whole * capacity :, :]
        last = jnp.concatenate([last[:, :, : LANES // 2], last[:, :, LANES // 2 :]], axis=1)
        pieces.append(last.reshape(slots, LANES // 2))
    cot = jnp.concatenate(pieces, axis=1)
    peak = jnp.zeros((1, LANES), jnp.float32)
    for pair in range(first // 2):
        tokens = jnp.concatenate([tile(2 * pair), tile(2 * pair + 1)], axis=1)
        product = lax.dot_general(cot, tokens, TN, preferred_element_type=jnp.float32)
        for side in range(2):
            block = product[:, side * LANES : (side + 1) * LANES]
            out_ref[2 * pair + side, :hidden] = block
            peak = jnp.maximum(peak, jnp.max(jnp.abs(block), axis=0, keepdims=True))
    peak = jnp.max(peak, axis=1, keepdims=True)
    power = jnp.clip(jnp.floor(jnp.log2(30000.0 / peak)), -100.0, 100.0)
    scale = jnp.exp2(power)
    for number in range(first):
        out_ref[number, :hidden] = out_ref[number, :hidden] * scale
        out_ref[number, hidden:] = jnp.broadcast_to(power, (TAG, LANES))


def gradients(arrived, width, hidden):
    return pl.pallas_call(
        functools.partial(gradient_kernel, width, hidden),
        out_shape=jax.ShapeDtypeStruct((width // LANES, hidden + TAG, LANES), jnp.float32),
        in_specs=[pl.BlockSpec(memory_space=pltpu.VMEM)],
        out_specs=pl.BlockSpec(memory_space=pltpu.VMEM),
        compiler_params=pltpu.CompilerParams(vmem_limit_bytes=40 * 2**20),
        name="gradient",
    )(arrived)


def newton_kernel(iters, gain, near_ref, far_ref, own_ref, out_ref):
    hidden = near_ref.shape[1]
    row = lax.broadcasted_iota(jnp.int32, (hidden, hidden), 0)
    col = lax.broadcasted_iota(jnp.int32, (hidden, hidden), 1)
    diag = row == col
    gram = near_ref[...] + lax.dot_general(
        far_ref[...], far_ref[...], TN, preferred_element_type=jnp.float32
    )
    total = jnp.sum(jnp.where(diag, gram, 0.0), keepdims=True)
    frobenius = jnp.sqrt(total) + norm_floor
    gram_iter = gram / (frobenius * frobenius)
    iterate = (own_ref[...].astype(jnp.float32) / frobenius).astype(jnp.bfloat16)
    for section in range(iters):
        narrow = gram_iter.astype(jnp.bfloat16)
        squared = jnp.dot(narrow, narrow, preferred_element_type=jnp.float32)
        polynomial = (jnp.where(diag, poly_first, 0.0) + poly_second * gram_iter + poly_third * squared).astype(jnp.bfloat16)
        product = jnp.dot(iterate, polynomial, preferred_element_type=jnp.float32)
        if section + 1 < iters:
            halfway = jnp.dot(narrow, polynomial, preferred_element_type=jnp.float32).astype(jnp.bfloat16)
            gram_iter = jnp.dot(halfway, polynomial, preferred_element_type=jnp.float32)
            iterate = product.astype(jnp.bfloat16)
    out_ref[...] = gain * product

def newton(near, far, own, iters, gain):
    return pl.pallas_call(
        functools.partial(newton_kernel, iters, gain),
        out_shape=jax.ShapeDtypeStruct(own.shape, jnp.float32),
        in_specs=[pl.BlockSpec(memory_space=pltpu.VMEM)]*3,
        out_specs=pl.BlockSpec(memory_space=pltpu.VMEM),
        compiler_params=pltpu.CompilerParams(vmem_limit_bytes=48*2**20),
        name="newton",
    )(near, far, own)


def from_half(parts, hidden):
    scale = jnp.exp2(parts[:, hidden : hidden + 1].astype(jnp.float32))
    return parts[:, :hidden].astype(jnp.float32) / scale


def placed(sizes, along):
    grid = np.arange(math.prod(sizes)).reshape(sizes)
    groups = []
    for core, axis in enumerate(along):
        part = np.moveaxis(grid[:, :, core, :], axis, -1)
        groups += part.reshape(-1, part.shape[-1]).tolist()
    return groups


def exchange(values, along):
    sizes = tuple(lax.axis_size(name) for name in ALL)
    return lax.all_to_all(
        values,
        ALL,
        split_axis=0,
        concat_axis=0,
        axis_index_groups=placed(sizes, along),
        tiled=True,
    )


def meet(rows):
    z, x, cores, y = (lax.axis_size(name) for name in ALL)
    own = rows.shape[0] // cores
    grid = np.arange(z * x * cores * y).reshape(z, x, cores, y)
    turned = np.transpose(grid, (3, 1, 2, 0))
    low = list(zip(grid[:, :, 0].ravel().tolist(), grid[:, :, 1].ravel().tolist()))
    low += list(zip(grid[:, :, 1].ravel().tolist(), turned[:, :, 0].ravel().tolist()))
    high = list(zip(grid[:, :, 1].ravel().tolist(), turned[:, :, 1].ravel().tolist()))
    zero = lax.axis_index("core") == 0
    crossing = lax.ppermute(jnp.where(zero, rows[own:], rows[:own]), ALL, low)
    across = lax.ppermute(rows[own:], ALL, high)
    return crossing + jnp.where(zero, rows[:own], across)


def body(tokens, routes, cotangents, momentum):
    groups = lax.axis_size("expert")
    cores = lax.axis_size("core")
    lines = lax.axis_size("x")
    chips = lax.axis_size("z") * lines
    tok_rows, width = tokens.shape
    hidden = cotangents.shape[2]
    capacity = 2 * tok_rows * routes.shape[1] // groups
    half = width // cores
    own = half // chips

    sent = pack(lax.axis_index("core"), routes, tokens, cotangents, groups, capacity, lines)
    with jax.named_scope("dispatch"):
        arrived = exchange(sent, (Y, Z))
    with jax.named_scope("gradient"):
        partial = gradients(arrived, width, hidden)
    with jax.named_scope("reduce"):
        parts = exchange(partial.astype(jnp.float16), (X, Y))
        line_sum = jnp.sum(from_half(parts, hidden), axis=0).T
        parts = exchange(line_sum.reshape(-1, cores * own, hidden), (Z, X))
        gradient = meet(jnp.sum(parts, axis=0))
    new_state = momentum_decay * momentum + gradient
    nesterov = (gradient + momentum_decay * new_state).astype(jnp.bfloat16)
    with jax.named_scope("gather"):
        spread = jnp.broadcast_to(nesterov[None], (chips, own, hidden))
        near = lax.all_to_all(spread, PLANE, split_axis=0, concat_axis=0, tiled=True)
        far = lax.ppermute(near, "core", SWAP).reshape(half, hidden)
        near = near.reshape(half, hidden)
        near_gram = lax.dot_general(near, near, TN, preferred_element_type=jnp.float32)
    gain = update_gain * math.sqrt(max(width, hidden))
    update = newton(near_gram, far, nesterov, ITERS, gain)
    return (new_state, update)


def solution(mesh):
    lines = mesh.devices.shape[1]
    fine = Mesh(mesh.devices.reshape(lines, lines, -1, lines), ALL)
    dp = ALL[:3]
    rows = ALL
    in_specs = (P(rows, None), P(rows, None), P(rows, None, None), P(dp, "expert"))
    out_specs = (P(dp, "expert"), P(dp, "expert"))
    return jax.shard_map(body, mesh=fine, in_specs=in_specs, out_specs=out_specs, check_vma=False)
```

```python
import functools
import math

import jax
import jax.numpy as jnp
import numpy as np
from jax import lax
from jax.experimental import pallas as pl
from jax.experimental.pallas import tpu as pltpu
from jax.sharding import Mesh, PartitionSpec as P

ITERS = 2


momentum_decay = 0.95
poly_first = 3.4445
poly_second = -4.775
poly_third = 2.0315
norm_floor = 1e-07
update_gain = 0.2

ALL = ("z", "x", "core", "expert")
Z, X, Y = 0, 1, 2
SWAP = [(0, 1), (1, 0)]
LANES = 128
TAG = 16
NT = (((1,), (1,)), ((), ()))
TN = (((0,), (0,)), ((), ()))


def pack_kernel(
    capacity, lines, core_ref, routes_hbm, tokens_hbm, cot_hbm, out_hbm, routes_ref, tokens_ref, cot_ref, out_ref, sems
):
    arrivals = [
        pltpu.make_async_copy(source, target, sems.at[number])
        for number, (source, target) in enumerate(
            ((routes_hbm, routes_ref), (tokens_hbm, tokens_ref), (cot_hbm, cot_ref))
        )
    ]
    for arrival in arrivals:
        arrival.start()
    top_count, rows = routes_ref.shape
    groups = out_ref.shape[0]
    slots = groups * capacity
    width = tokens_ref.shape[1]
    rest = width // (lines * lines)
    source = lax.broadcasted_iota(jnp.int32, (width, width), 0)
    target = lax.broadcasted_iota(jnp.int32, (1, width), 1)
    first = target // (lines * rest)
    second = target // rest % lines
    place = jnp.where(core_ref[0] == 0, second * lines + first, first * lines + second)
    wanted = place * rest + target % rest
    order = (source == wanted).astype(jnp.float32).astype(jnp.bfloat16)
    names = lax.broadcasted_iota(jnp.int32, (groups, rows), 0)
    before = (
        lax.broadcasted_iota(jnp.int32, (rows, rows), 0)
        < lax.broadcasted_iota(jnp.int32, (rows, rows), 1)
    ).astype(jnp.bfloat16)
    places = lax.broadcasted_iota(jnp.int32, (slots, rows), 0)
    count = jnp.zeros((groups, 1), jnp.float32)
    chosen = []
    arrivals[0].wait()
    for k in range(top_count):
        route = routes_ref[k:k+1, :]
        member = (names == route).astype(jnp.float32)
        earlier = jnp.dot(member.astype(jnp.bfloat16), before, preferred_element_type=jnp.float32) + count
        position = jnp.sum(earlier * member, axis=0, keepdims=True).astype(jnp.int32)
        count = count + jnp.sum(member, axis=1, keepdims=True)
        chosen.append((places == route * capacity + position).astype(jnp.float32).astype(jnp.bfloat16))
    arrivals[2].wait()
    picked = lax.dot_general(chosen[0], cot_ref[0], NT, preferred_element_type=jnp.float32)
    for k in range(1, top_count):
        picked = picked + lax.dot_general(
            chosen[k], cot_ref[k], NT, preferred_element_type=jnp.float32
        )
    picked = picked.astype(jnp.bfloat16)
    hidden = picked.shape[1]
    start = width // LANES * capacity
    for tile in range(hidden // LANES):
        part = picked[:, tile * LANES : (tile + 1) * LANES].reshape(groups, capacity, LANES)
        out_ref[:, start : start + capacity, :] = part
        start += capacity
    rest_columns = hidden % LANES
    if rest_columns:
        part = picked[:, hidden - rest_columns :].reshape(groups, capacity, rest_columns)
        out_ref[:, start:, :] = jnp.concatenate(
            [part[:, : capacity // 2], part[:, capacity // 2 :]], axis=2
        )

    def leave(begin, end, number):
        departure = pltpu.make_async_copy(
            out_ref.at[:, begin:end, :], out_hbm.at[:, begin:end, :], sems.at[number]
        )
        departure.start()
        return departure

    first = width // LANES * capacity
    departures = [leave(first, out_ref.shape[1], 3)]
    arrivals[1].wait()
    by_core = jnp.dot(
        tokens_ref[...], order, preferred_element_type=jnp.float32
    ).astype(jnp.bfloat16)
    by_token = chosen[0]
    for k in range(1, top_count):
        by_token = by_token + chosen[k]
    middle = width // 2
    for side in range(2):
        sent = jnp.dot(
            by_token,
            by_core[:, side * middle : (side + 1) * middle],
            preferred_element_type=jnp.float32,
        ).astype(jnp.bfloat16)
        for tile in range(middle // LANES):
            begin = side * first // 2 + tile * capacity
            part = sent[:, tile * LANES : (tile + 1) * LANES].reshape(groups, capacity, LANES)
            out_ref[:, begin : begin + capacity, :] = part
        departures.append(leave(side * first // 2, (side + 1) * first // 2, 4 + side))
    for departure in departures:
        departure.wait()


def pack(core, routes, tokens, cotangents, groups, capacity, lines):
    rows, width = tokens.shape
    _, top, hidden = cotangents.shape
    filled = capacity * (width + hidden) // LANES
    return pl.pallas_call(
        functools.partial(pack_kernel, capacity, lines),
        out_shape=jax.ShapeDtypeStruct((groups, filled, LANES), jnp.bfloat16),
        in_specs=[pl.BlockSpec(memory_space=pltpu.SMEM)] + [pl.BlockSpec(memory_space=pl.ANY)] * 3,
        out_specs=pl.BlockSpec(memory_space=pl.ANY),
        scratch_shapes=[
            pltpu.VMEM((top, rows), jnp.int32),
            pltpu.VMEM((rows, width), jnp.bfloat16),
            pltpu.VMEM((top, hidden, rows), jnp.bfloat16),
            pltpu.VMEM((groups, filled, LANES), jnp.bfloat16),
            pltpu.SemaphoreType.DMA((6,)),
        ],
        compiler_params=pltpu.CompilerParams(vmem_limit_bytes=60 * 2**20),
        name="pack",
    )(core.reshape(1), routes.T, tokens, jnp.transpose(cotangents,(1,2,0)))

def gradient_kernel(width, hidden, arrived_ref, out_ref):
    groups, filled, _ = arrived_ref.shape
    capacity = filled * LANES // (width + hidden)
    slots = groups * capacity

    def tile(number):
        part = arrived_ref[:, number * capacity : (number + 1) * capacity, :]
        return part.reshape(slots, LANES)

    first = width // LANES
    whole = filled // capacity
    pieces = [tile(number) for number in range(first, whole)]
    if filled % capacity:
        last = arrived_ref[:, whole * capacity :, :]
        last = jnp.concatenate([last[:, :, : LANES // 2], last[:, :, LANES // 2 :]], axis=1)
        pieces.append(last.reshape(slots, LANES // 2))
    cot = jnp.concatenate(pieces, axis=1)
    peak = jnp.zeros((1, LANES), jnp.float32)
    for pair in range(first // 2):
        tokens = jnp.concatenate([tile(2 * pair), tile(2 * pair + 1)], axis=1)
        product = lax.dot_general(cot, tokens, TN, preferred_element_type=jnp.float32)
        for side in range(2):
            block = product[:, side * LANES : (side + 1) * LANES]
            out_ref[2 * pair + side, :hidden] = block
            peak = jnp.maximum(peak, jnp.max(jnp.abs(block), axis=0, keepdims=True))
    peak = jnp.max(peak, axis=1, keepdims=True)
    power = jnp.clip(jnp.floor(jnp.log2(30000.0 / peak)), -100.0, 100.0)
    scale = jnp.exp2(power)
    for number in range(first):
        out_ref[number, :hidden] = out_ref[number, :hidden] * scale
        out_ref[number, hidden:] = jnp.broadcast_to(power, (TAG, LANES))


def gradients(arrived, width, hidden):
    return pl.pallas_call(
        functools.partial(gradient_kernel, width, hidden),
        out_shape=jax.ShapeDtypeStruct((width // LANES, hidden + TAG, LANES), jnp.float32),
        in_specs=[pl.BlockSpec(memory_space=pltpu.VMEM)],
        out_specs=pl.BlockSpec(memory_space=pltpu.VMEM),
        compiler_params=pltpu.CompilerParams(vmem_limit_bytes=40 * 2**20),
        name="gradient",
    )(arrived)


def newton_kernel(iters, gain, near_ref, far_ref, own_ref, out_ref):
    hidden = near_ref.shape[1]
    row = lax.broadcasted_iota(jnp.int32, (hidden, hidden), 0)
    col = lax.broadcasted_iota(jnp.int32, (hidden, hidden), 1)
    diag = row == col
    gram = near_ref[...] + lax.dot_general(
        far_ref[...], far_ref[...], TN, preferred_element_type=jnp.float32
    )
    total = jnp.sum(jnp.where(diag, gram, 0.0), keepdims=True)
    frobenius = jnp.sqrt(total) + norm_floor
    gram_iter = gram / (frobenius * frobenius)
    iterate = (own_ref[...].astype(jnp.float32) / frobenius).astype(jnp.bfloat16)
    for section in range(iters):
        narrow = gram_iter.astype(jnp.bfloat16)
        squared = jnp.dot(narrow, narrow, preferred_element_type=jnp.float32)
        polynomial = (jnp.where(diag, poly_first, 0.0) + poly_second * gram_iter + poly_third * squared).astype(jnp.bfloat16)
        product = jnp.dot(iterate, polynomial, preferred_element_type=jnp.float32)
        if section + 1 < iters:
            halfway = jnp.dot(narrow, polynomial, preferred_element_type=jnp.float32).astype(jnp.bfloat16)
            gram_iter = jnp.dot(halfway, polynomial, preferred_element_type=jnp.float32)
            iterate = product.astype(jnp.bfloat16)
    out_ref[...] = gain * product

def newton(near, far, own, iters, gain):
    return pl.pallas_call(
        functools.partial(newton_kernel, iters, gain),
        out_shape=jax.ShapeDtypeStruct(own.shape, jnp.float32),
        in_specs=[pl.BlockSpec(memory_space=pltpu.VMEM)]*3,
        out_specs=pl.BlockSpec(memory_space=pltpu.VMEM),
        compiler_params=pltpu.CompilerParams(vmem_limit_bytes=48*2**20),
        name="newton",
    )(near, far, own)


def from_half(parts, hidden):
    scale = jnp.exp2(parts[:, hidden : hidden + 1].astype(jnp.float32))
    return parts[:, :hidden].astype(jnp.float32) / scale


def placed(sizes, along):
    grid = np.arange(math.prod(sizes)).reshape(sizes)
    groups = []
    for core, axis in enumerate(along):
        part = np.moveaxis(grid[:, :, core, :], axis, -1)
        groups += part.reshape(-1, part.shape[-1]).tolist()
    return groups


def exchange(values, along):
    sizes = tuple(lax.axis_size(name) for name in ALL)
    return lax.all_to_all(
        values,
        ALL,
        split_axis=0,
        concat_axis=0,
        axis_index_groups=placed(sizes, along),
        tiled=True,
    )


def meet(rows):
    z, x, cores, y = (lax.axis_size(name) for name in ALL)
    own = rows.shape[0] // cores
    grid = np.arange(z * x * cores * y).reshape(z, x, cores, y)
    turned = np.transpose(grid, (3, 1, 2, 0))
    low = list(zip(grid[:, :, 0].ravel().tolist(), grid[:, :, 1].ravel().tolist()))
    low += list(zip(grid[:, :, 1].ravel().tolist(), turned[:, :, 0].ravel().tolist()))
    high = list(zip(grid[:, :, 1].ravel().tolist(), turned[:, :, 1].ravel().tolist()))
    zero = lax.axis_index("core") == 0
    crossing = lax.ppermute(jnp.where(zero, rows[own:], rows[:own]), ALL, low)
    across = lax.ppermute(rows[own:], ALL, high)
    return crossing + jnp.where(zero, rows[:own], across)


def body(tokens, routes, cotangents, momentum):
    groups = lax.axis_size("expert")
    cores = lax.axis_size("core")
    lines = lax.axis_size("x")
    chips = lax.axis_size("z") * lines
    tok_rows, width = tokens.shape
    hidden = cotangents.shape[2]
    capacity = 2 * tok_rows * routes.shape[1] // groups
    half = width // cores
    own = half // chips

    sent = pack(lax.axis_index("core"), routes, tokens, cotangents, groups, capacity, lines)
    with jax.named_scope("dispatch"):
        arrived = exchange(sent, (Y, Z))
    with jax.named_scope("gradient"):
        partial = gradients(arrived, width, hidden)
    with jax.named_scope("reduce"):
        parts = exchange(partial.astype(jnp.float16), (X, Y))
        line_sum = jnp.sum(from_half(parts, hidden), axis=0).T
        parts = exchange(line_sum.reshape(-1, cores * own, hidden), (Z, X))
        gradient = meet(jnp.sum(parts, axis=0))
    new_state = momentum_decay * momentum + gradient
    nesterov = (gradient + momentum_decay * new_state).astype(jnp.bfloat16)
    with jax.named_scope("gather"):
        spread = jnp.broadcast_to(nesterov[None], (lines, own, hidden))
        line = exchange(spread, (Z, X)).reshape(lines * own, hidden)
        spread = jnp.broadcast_to(line[None], (lines, lines * own, hidden))
        near = exchange(spread, (X, Z)).reshape(chips, own, hidden)
        far = lax.ppermute(near, "core", SWAP).reshape(half, hidden)
        near = near.reshape(half, hidden)
        near_gram = lax.dot_general(near, near, TN, preferred_element_type=jnp.float32)
    gain = update_gain * math.sqrt(max(width, hidden))
    update = newton(near_gram, far, nesterov, ITERS, gain)
    return (new_state, update)


def solution(mesh):
    lines = mesh.devices.shape[1]
    fine = Mesh(mesh.devices.reshape(lines, lines, -1, lines), ALL)
    dp = ALL[:3]
    rows = ALL
    in_specs = (P(rows, None), P(rows, None), P(rows, None, None), P(dp, "expert"))
    out_specs = (P(dp, "expert"), P(dp, "expert"))
    return jax.shard_map(body, mesh=fine, in_specs=in_specs, out_specs=out_specs, check_vma=False)
```

```python
import functools
import math

import jax
import jax.numpy as jnp
import numpy as np
from jax import lax
from jax.experimental import pallas as pl
from jax.experimental.pallas import tpu as pltpu
from jax.sharding import Mesh, PartitionSpec as P

ITERS = 2


momentum_decay = 0.95
poly_first = 3.4445
poly_second = -4.775
poly_third = 2.0315
norm_floor = 1e-07
update_gain = 0.2

ALL = ("z", "x", "core", "expert")
Z, X, Y = 0, 1, 2
PLANE = ("z", "x")
SWAP = [(0, 1), (1, 0)]
LANES = 128
TAG = 16
NT = (((1,), (1,)), ((), ()))
TN = (((0,), (0,)), ((), ()))


def pack_kernel(
    capacity, lines, core_ref, routes_hbm, tokens_hbm, cot_hbm, out_hbm, routes_ref, tokens_ref, cot_ref, out_ref, sems
):
    arrivals = [
        pltpu.make_async_copy(source, target, sems.at[number])
        for number, (source, target) in enumerate(
            ((routes_hbm, routes_ref), (tokens_hbm, tokens_ref), (cot_hbm, cot_ref))
        )
    ]
    for arrival in arrivals:
        arrival.start()
    top_count, rows = routes_ref.shape
    groups = out_ref.shape[0]
    slots = groups * capacity
    width = tokens_ref.shape[1]
    rest = width // (lines * lines)
    source = lax.broadcasted_iota(jnp.int32, (width, width), 0)
    target = lax.broadcasted_iota(jnp.int32, (width, width), 1)
    first = target // (lines * rest)
    second = target // rest % lines
    place = jnp.where(core_ref[0] == 0, second * lines + first, first * lines + second)
    wanted = place * rest + target % rest
    order = (source == wanted).astype(jnp.float32).astype(jnp.bfloat16)
    names = lax.broadcasted_iota(jnp.int32, (groups, rows), 0)
    before = (
        lax.broadcasted_iota(jnp.int32, (rows, rows), 0)
        < lax.broadcasted_iota(jnp.int32, (rows, rows), 1)
    ).astype(jnp.bfloat16)
    places = lax.broadcasted_iota(jnp.int32, (slots, rows), 0)
    count = jnp.zeros((groups, 1), jnp.float32)
    chosen = []
    arrivals[0].wait()
    for k in range(top_count):
        route = routes_ref[k:k+1, :]
        member = (names == route).astype(jnp.float32)
        earlier = jnp.dot(member.astype(jnp.bfloat16), before, preferred_element_type=jnp.float32) + count
        position = jnp.sum(earlier * member, axis=0, keepdims=True).astype(jnp.int32)
        count = count + jnp.sum(member, axis=1, keepdims=True)
        chosen.append((places == route * capacity + position).astype(jnp.float32).astype(jnp.bfloat16))
    arrivals[2].wait()
    picked = lax.dot_general(chosen[0], cot_ref[0], NT, preferred_element_type=jnp.float32)
    for k in range(1, top_count):
        picked = picked + lax.dot_general(
            chosen[k], cot_ref[k], NT, preferred_element_type=jnp.float32
        )
    picked = picked.astype(jnp.bfloat16)
    hidden = picked.shape[1]
    start = width // LANES * capacity
    for tile in range(hidden // LANES):
        part = picked[:, tile * LANES : (tile + 1) * LANES].reshape(groups, capacity, LANES)
        out_ref[:, start : start + capacity, :] = part
        start += capacity
    rest_columns = hidden % LANES
    if rest_columns:
        part = picked[:, hidden - rest_columns :].reshape(groups, capacity, rest_columns)
        out_ref[:, start:, :] = jnp.concatenate(
            [part[:, : capacity // 2], part[:, capacity // 2 :]], axis=2
        )

    def leave(begin, end, number):
        departure = pltpu.make_async_copy(
            out_ref.at[:, begin:end, :], out_hbm.at[:, begin:end, :], sems.at[number]
        )
        departure.start()
        return departure

    first = width // LANES * capacity
    departures = [leave(first, out_ref.shape[1], 3)]
    arrivals[1].wait()
    by_core = jnp.dot(
        tokens_ref[...], order, preferred_element_type=jnp.float32
    ).astype(jnp.bfloat16)
    by_token = chosen[0]
    for k in range(1, top_count):
        by_token = by_token + chosen[k]
    middle = width // 2
    for side in range(2):
        sent = jnp.dot(
            by_token,
            by_core[:, side * middle : (side + 1) * middle],
            preferred_element_type=jnp.float32,
        ).astype(jnp.bfloat16)
        for tile in range(middle // LANES):
            begin = side * first // 2 + tile * capacity
            part = sent[:, tile * LANES : (tile + 1) * LANES].reshape(groups, capacity, LANES)
            out_ref[:, begin : begin + capacity, :] = part
        departures.append(leave(side * first // 2, (side + 1) * first // 2, 4 + side))
    for departure in departures:
        departure.wait()


def pack(core, routes, tokens, cotangents, groups, capacity, lines):
    rows, width = tokens.shape
    _, top, hidden = cotangents.shape
    filled = capacity * (width + hidden) // LANES
    return pl.pallas_call(
        functools.partial(pack_kernel, capacity, lines),
        out_shape=jax.ShapeDtypeStruct((groups, filled, LANES), jnp.bfloat16),
        in_specs=[pl.BlockSpec(memory_space=pltpu.SMEM)] + [pl.BlockSpec(memory_space=pl.ANY)] * 3,
        out_specs=pl.BlockSpec(memory_space=pl.ANY),
        scratch_shapes=[
            pltpu.VMEM((top, rows), jnp.int32),
            pltpu.VMEM((rows, width), jnp.bfloat16),
            pltpu.VMEM((top, hidden, rows), jnp.bfloat16),
            pltpu.VMEM((groups, filled, LANES), jnp.bfloat16),
            pltpu.SemaphoreType.DMA((6,)),
        ],
        compiler_params=pltpu.CompilerParams(vmem_limit_bytes=60 * 2**20),
        name="pack",
    )(core.reshape(1), routes.T, tokens, jnp.transpose(cotangents,(1,2,0)))

def gradient_kernel(width, hidden, arrived_ref, out_ref):
    groups, filled, _ = arrived_ref.shape
    capacity = filled * LANES // (width + hidden)
    slots = groups * capacity

    def tile(number):
        part = arrived_ref[:, number * capacity : (number + 1) * capacity, :]
        return part.reshape(slots, LANES)

    first = width // LANES
    whole = filled // capacity
    pieces = [tile(number) for number in range(first, whole)]
    if filled % capacity:
        last = arrived_ref[:, whole * capacity :, :]
        last = jnp.concatenate([last[:, :, : LANES // 2], last[:, :, LANES // 2 :]], axis=1)
        pieces.append(last.reshape(slots, LANES // 2))
    cot = jnp.concatenate(pieces, axis=1)
    peak = jnp.zeros((1, LANES), jnp.float32)
    for pair in range(first // 2):
        tokens = jnp.concatenate([tile(2 * pair), tile(2 * pair + 1)], axis=1)
        product = lax.dot_general(cot, tokens, TN, preferred_element_type=jnp.float32)
        for side in range(2):
            block = product[:, side * LANES : (side + 1) * LANES]
            out_ref[2 * pair + side, :hidden] = block
            peak = jnp.maximum(peak, jnp.max(jnp.abs(block), axis=0, keepdims=True))
    peak = jnp.max(peak, axis=1, keepdims=True)
    power = jnp.clip(jnp.floor(jnp.log2(30000.0 / peak)), -100.0, 100.0)
    scale = jnp.exp2(power)
    for number in range(first):
        out_ref[number, :hidden] = out_ref[number, :hidden] * scale
        out_ref[number, hidden:] = jnp.broadcast_to(power, (TAG, LANES))


def gradients(arrived, width, hidden):
    return pl.pallas_call(
        functools.partial(gradient_kernel, width, hidden),
        out_shape=jax.ShapeDtypeStruct((width // LANES, hidden + TAG, LANES), jnp.float32),
        in_specs=[pl.BlockSpec(memory_space=pltpu.VMEM)],
        out_specs=pl.BlockSpec(memory_space=pltpu.VMEM),
        compiler_params=pltpu.CompilerParams(vmem_limit_bytes=40 * 2**20),
        name="gradient",
    )(arrived)


def turn_kernel(source_ref, target_ref):
    target_ref[...] = source_ref[...].T


def turn(values):
    return pl.pallas_call(
        turn_kernel,
        out_shape=jax.ShapeDtypeStruct(values.shape[::-1], values.dtype),
        in_specs=[pl.BlockSpec(memory_space=pltpu.VMEM)],
        out_specs=pl.BlockSpec(memory_space=pltpu.VMEM),
        name="turn",
    )(values)


def newton_kernel(iters, gain, near_ref, far_ref, own_ref, out_ref):
    hidden = near_ref.shape[1]
    row = lax.broadcasted_iota(jnp.int32, (hidden, hidden), 0)
    col = lax.broadcasted_iota(jnp.int32, (hidden, hidden), 1)
    diag = row == col
    gram = near_ref[...] + lax.dot_general(
        far_ref[...], far_ref[...], TN, preferred_element_type=jnp.float32
    )
    total = jnp.sum(jnp.where(diag, gram, 0.0), keepdims=True)
    frobenius = jnp.sqrt(total) + norm_floor
    gram_iter = gram / (frobenius * frobenius)
    iterate = (own_ref[...].astype(jnp.float32) / frobenius).astype(jnp.bfloat16)
    for section in range(iters):
        narrow = gram_iter.astype(jnp.bfloat16)
        squared = jnp.dot(narrow, narrow, preferred_element_type=jnp.float32)
        polynomial = (jnp.where(diag, poly_first, 0.0) + poly_second * gram_iter + poly_third * squared).astype(jnp.bfloat16)
        product = jnp.dot(iterate, polynomial, preferred_element_type=jnp.float32)
        if section + 1 < iters:
            halfway = jnp.dot(narrow, polynomial, preferred_element_type=jnp.float32).astype(jnp.bfloat16)
            gram_iter = jnp.dot(halfway, polynomial, preferred_element_type=jnp.float32)
            iterate = product.astype(jnp.bfloat16)
    out_ref[...] = gain * product

def newton(near, far, own, iters, gain):
    return pl.pallas_call(
        functools.partial(newton_kernel, iters, gain),
        out_shape=jax.ShapeDtypeStruct(own.shape, jnp.float32),
        in_specs=[pl.BlockSpec(memory_space=pltpu.VMEM)]*3,
        out_specs=pl.BlockSpec(memory_space=pltpu.VMEM),
        compiler_params=pltpu.CompilerParams(vmem_limit_bytes=48*2**20),
        name="newton",
    )(near, far, own)


def from_half(parts, hidden):
    scale = jnp.exp2(parts[:, hidden : hidden + 1].astype(jnp.float32))
    return parts[:, :hidden].astype(jnp.float32) / scale


def placed(sizes, along):
    grid = np.arange(math.prod(sizes)).reshape(sizes)
    groups = []
    for core, axis in enumerate(along):
        part = np.moveaxis(grid[:, :, core, :], axis, -1)
        groups += part.reshape(-1, part.shape[-1]).tolist()
    return groups


def exchange(values, along):
    sizes = tuple(lax.axis_size(name) for name in ALL)
    return lax.all_to_all(
        values,
        ALL,
        split_axis=0,
        concat_axis=0,
        axis_index_groups=placed(sizes, along),
        tiled=True,
    )


def meet(rows):
    z, x, cores, y = (lax.axis_size(name) for name in ALL)
    own = rows.shape[0] // cores
    grid = np.arange(z * x * cores * y).reshape(z, x, cores, y)
    turned = np.transpose(grid, (3, 1, 2, 0))
    low = list(zip(grid[:, :, 0].ravel().tolist(), grid[:, :, 1].ravel().tolist()))
    low += list(zip(grid[:, :, 1].ravel().tolist(), turned[:, :, 0].ravel().tolist()))
    high = list(zip(grid[:, :, 1].ravel().tolist(), turned[:, :, 1].ravel().tolist()))
    zero = lax.axis_index("core") == 0
    crossing = lax.ppermute(jnp.where(zero, rows[own:], rows[:own]), ALL, low)
    across = lax.ppermute(rows[own:], ALL, high)
    return crossing + jnp.where(zero, rows[:own], across)


def body(tokens, routes, cotangents, momentum):
    groups = lax.axis_size("expert")
    cores = lax.axis_size("core")
    lines = lax.axis_size("x")
    chips = lax.axis_size("z") * lines
    tok_rows, width = tokens.shape
    hidden = cotangents.shape[2]
    capacity = 2 * tok_rows * routes.shape[1] // groups
    half = width // cores
    own = half // chips

    sent = pack(lax.axis_index("core"), routes, tokens, cotangents, groups, capacity, lines)
    with jax.named_scope("dispatch"):
        arrived = exchange(sent, (Y, Z))
    with jax.named_scope("gradient"):
        partial = gradients(arrived, width, hidden)
    with jax.named_scope("reduce"):
        parts = exchange(partial.astype(jnp.float16), (X, Y))
        line_sum = turn(jnp.sum(from_half(parts, hidden), axis=0))
        parts = exchange(line_sum.reshape(-1, cores * own, hidden), (Z, X))
        gradient = meet(jnp.sum(parts, axis=0))
    new_state = momentum_decay * momentum + gradient
    nesterov = (gradient + momentum_decay * new_state).astype(jnp.bfloat16)
    with jax.named_scope("gather"):
        spread = jnp.broadcast_to(nesterov[None], (chips, own, hidden))
        near = lax.all_to_all(spread, PLANE, split_axis=0, concat_axis=0, tiled=True)
        far = lax.ppermute(near, "core", SWAP).reshape(half, hidden)
        near = near.reshape(half, hidden)
        near_gram = lax.dot_general(near, near, TN, preferred_element_type=jnp.float32)
    gain = update_gain * math.sqrt(max(width, hidden))
    update = newton(near_gram, far, nesterov, ITERS, gain)
    return (new_state, update)


def solution(mesh):
    lines = mesh.devices.shape[1]
    fine = Mesh(mesh.devices.reshape(lines, lines, -1, lines), ALL)
    dp = ALL[:3]
    rows = ALL
    in_specs = (P(rows, None), P(rows, None), P(rows, None, None), P(dp, "expert"))
    out_specs = (P(dp, "expert"), P(dp, "expert"))
    return jax.shard_map(body, mesh=fine, in_specs=in_specs, out_specs=out_specs, check_vma=False)
```
